128 devices in a mesh: inst: 4 (over y), ctx: 16 (over z, x), head: 2 (over core).
Axes of the slice: x: 4, y: 4, z: 4, core: 2. Of those that a mesh axis runs over, the one named last changes fastest.
Arguments:
- cache: bfloat16 [2, 32, 8192, 1024], P(None, 'inst', 'ctx', 'head'), may hold values from -600 to 600, as said below
- hidden: bfloat16 [3, 32, 6144], P(None, 'inst', 'ctx'), may hold values from -14 to 14
- norm_gain: bfloat16 [6144], P('ctx'), may hold values from 0.099609375 to 1.8984375
- w_query: bfloat16 [6144, 6144], P('ctx', 'head'), may hold values from -0.078125 to 0.078125
- key_value_weight: bfloat16 [2, 6144, 1024], P(None, 'ctx', 'head'), may hold values from -0.078125 to 0.078125
- w_out: bfloat16 [6144, 6144], P('head', 'ctx'), may hold values from -0.078125 to 0.078125
- lengths: int32 [32], replicated, may hold values from 0 to 8189, as said below
- dest_inst: int32 [8], replicated, may hold values from 0 to 2, as said below
- dest_slot: int32 [8], replicated, may hold values from 0 to 7, as said below
- block_order: int32 [256], replicated, may hold values from 0 to 255, as said below
Outputs:
- new_cache: bfloat16 [2, 32, 8192, 1024], P(None, 'inst', 'ctx', 'head')
- attn_out: bfloat16 [3, 32, 6144], P(None, 'inst', ('ctx', 'head'))
The draws below stay inside these ranges and needn't reach their ends.
Inputs may be any that keep to these rules, and one draw needn't show every extreme that they name: `cache`: keys and values; the retiring instance 4 - 1 keeps its slots in the block order of block_order, the others in position order. `lengths`: 0 marks a free slot; every slot of instance 4 - 1 holds a request; each instance below it has exactly as many free slots as requests that move to it; some request has exactly 8189. `dest_inst`: no instance takes more than 3 requests, and some instance takes exactly 3. The pairs of dest_inst and dest_slot are distinct and name free slots. A permutation of the 256 blocks of 32 positions; stored block j holds logical positions block_order[j] * 32 onward; the 16 blocks stored on one ctx device belong to the ranges of 16 different ctx devices, range c being blocks c * 16 to c * 16 + 15.
All inputs are finite; a program needn't handle non-finite values.
Results may differ from the reference program's by a relative error of at most 0.02.
The reference program's roundings to bfloat16 on the way count: a program that leaves them out, or rounds other values in their place, can miss the bound.
Values may be sent and summed in bfloat16 or wider, within the bound.
No kernel may reach another device: no remote copies, remote signals or barrier semaphores. Data moves between devices by JAX's collectives and lax.ppermute only.
A program may use at most 128 MiB of HBM per device.

```python
import jax
import jax.numpy as jnp
from jax import lax

MODEL_WIDTH = 6144
QUERY_HEADS = 48
KEY_HEADS = 8
HEAD_SIZE = 128
SLOTS = 8
TOKEN_STEPS = 3
CACHE_LENGTH = 8192
GLOBAL_SLOTS = 32
N_INST = 4
N_CTX = 16


def plan_tables(key):
    receivers = N_INST - 1
    turn_key, recv_key, slot_key = jax.random.split(key, 3)
    turn = jax.random.permutation(turn_key, SLOTS).astype(jnp.int32)
    recv_perm = jax.random.permutation(recv_key, receivers).astype(jnp.int32)
    dest_inst = recv_perm[turn % receivers]
    rank = turn // receivers
    slot_perms = jax.vmap(lambda sub_key: jax.random.permutation(sub_key, SLOTS))(jax.random.split(slot_key, N_INST)).astype(jnp.int32)
    dest_slot = slot_perms[dest_inst, rank]
    return (turn, dest_inst.astype(jnp.int32), dest_slot.astype(jnp.int32), slot_perms)


def draw_dest_inst(key, part):
    return plan_tables(key)[1]


def draw_dest_slot(key, part):
    return plan_tables(key)[2]


def draw_lengths(key, part):
    turn, dest_inst, dest_slot, slot_perms = plan_tables(key)
    key = jax.random.fold_in(key, 11)
    instances = jnp.arange(N_INST, dtype=jnp.int32)
    counts = jnp.sum((dest_inst[None, :] == instances[:, None]).astype(jnp.int32), axis=1)
    ranks = jnp.arange(SLOTS, dtype=jnp.int32)
    slot_ids = jnp.arange(SLOTS, dtype=jnp.int32)
    hits = (slot_perms[:, :, None] == slot_ids[None, None, :]) & (ranks[None, :, None] < counts[:, None, None])
    free_slots = jnp.any(hits, axis=1).reshape(-1)
    raw = jax.random.randint(key, (GLOBAL_SLOTS,), 1, CACHE_LENGTH - TOKEN_STEPS + 1).astype(jnp.int32)
    first_request = jnp.sum(jnp.arange(SLOTS, dtype=jnp.int32) * (turn == 0).astype(jnp.int32))
    top_slot = (N_INST - 1) * SLOTS + first_request
    raw = jnp.where(jnp.arange(GLOBAL_SLOTS, dtype=jnp.int32) == top_slot, CACHE_LENGTH - TOKEN_STEPS, raw)
    return jnp.where(free_slots, 0, raw).astype(jnp.int32)


def draw_block_order(key, part):
    key = jax.random.fold_in(key, 7)
    dest_key, sub_key = jax.random.split(key)
    dest = jax.vmap(lambda one_key: jax.random.permutation(one_key, N_CTX))(jax.random.split(dest_key, N_CTX)).astype(jnp.int32)
    sub = jax.vmap(lambda one_key: jax.random.permutation(one_key, N_CTX))(jax.random.split(sub_key, N_CTX)).astype(jnp.int32)
    sources = jnp.arange(N_CTX, dtype=jnp.int32)[:, None]
    layout = dest * N_CTX + sub[dest, sources]
    return layout.reshape(-1).astype(jnp.int32)


def draw_hidden(key, part):
    key = jax.random.fold_in(key, 5)
    column = jnp.arange(MODEL_WIDTH, dtype=jnp.float32) / MODEL_WIDTH
    ramp = 0.6 * jnp.exp(column * jnp.log(3.0))
    array_shape = (TOKEN_STEPS, GLOBAL_SLOTS, MODEL_WIDTH)
    cached_values = jnp.clip(jax.random.normal(key, array_shape, jnp.float32), -5.0, 5.0) * ramp
    return cached_values.astype(jnp.bfloat16)


def draw_cache(key, part):
    key = jax.random.fold_in(key, 3)
    array_shape = (2, GLOBAL_SLOTS, CACHE_LENGTH, KEY_HEADS * HEAD_SIZE)
    cached_values = jnp.clip(jax.random.normal(key, array_shape, jnp.float32), -6.0, 6.0)
    return cached_values.astype(jnp.bfloat16)


def block_scale(stream_key, extent, cuts, least, largest):
    def one(axis_at, shards_of):
        steps = jax.random.uniform(jax.random.fold_in(jax.random.fold_in(stream_key, 6), axis_at), (shards_of,), jnp.float32, least / len(cuts), largest / len(cuts))
        return jnp.repeat(jnp.exp(steps), extent[axis_at] // shards_of).reshape((-1,) + (1,) * (len(extent) - axis_at - 1))

    gain = one(*cuts[0])
    for cut in cuts[1:]:
        gain = gain * one(*cut)
    return gain


def noise(own_key, shape, deviation, bound, pieces=(), kind=jnp.bfloat16):
    gain = block_scale(own_key, shape, pieces, -0.22, 0.18) if pieces else 1.0
    result = jax.random.normal(own_key, shape, jnp.float32) * deviation * gain
    return jnp.minimum(jnp.maximum(result, -bound), bound).astype(kind)


def setup_inputs(seed: int = 0) -> dict:
    key_list = jax.random.split(jax.random.key(seed), 11)
    cache = draw_cache(jax.random.fold_in(key_list[10], 71), 0)
    hidden = draw_hidden(jax.random.fold_in(key_list[10], 71), 0)
    norm_gain = jnp.clip(1.0 + 0.18 * jax.random.normal(key_list[2], (MODEL_WIDTH,), jnp.float32), 0.099609375, 1.8984375).astype(jnp.bfloat16)
    w_query = noise(key_list[3], (MODEL_WIDTH, QUERY_HEADS * HEAD_SIZE), MODEL_WIDTH ** -0.5, 0.078125, ((0, 16), (1, 2)))
    key_value_weight = noise(key_list[4], (2, MODEL_WIDTH, KEY_HEADS * HEAD_SIZE), MODEL_WIDTH ** -0.5, 0.078125, ((1, 16), (2, 2)))
    w_out = noise(key_list[5], (QUERY_HEADS * HEAD_SIZE, MODEL_WIDTH), (QUERY_HEADS * HEAD_SIZE) ** -0.5, 0.078125, ((0, 2), (1, 16)))
    lengths = draw_lengths(jax.random.fold_in(key_list[10], 71), 0)
    dest_inst = draw_dest_inst(jax.random.fold_in(key_list[10], 71), 0)
    dest_slot = draw_dest_slot(jax.random.fold_in(key_list[10], 71), 0)
    block_order = draw_block_order(jax.random.fold_in(key_list[10], 71), 0)
    return {"cache": cache, "hidden": hidden, "norm_gain": norm_gain, "w_query": w_query, "key_value_weight": key_value_weight, "w_out": w_out, "lengths": lengths, "dest_inst": dest_inst, "dest_slot": dest_slot, "block_order": block_order}


ROPE_BASE = 500000.0
NORM_EPSILON = 1e-05
MASKED_SCORE = -1e+30

def apply_rotary(vector, position):
    half_dim = vector.shape[-1] // 2
    frequency = ROPE_BASE ** (-jnp.arange(half_dim, dtype=jnp.float32) * 2.0 / vector.shape[-1])
    angles = position.astype(jnp.float32)[..., None, None] * frequency
    cosine = jnp.cos(angles)
    sine = jnp.sin(angles)
    front_half = vector[..., :half_dim]
    second = vector[..., half_dim:]
    return jnp.concatenate([front_half * cosine - second * sine, second * cosine + front_half * sine], axis=-1)

def reference(cache, hidden, norm_gain, w_query, key_value_weight, w_out, lengths, dest_inst, dest_slot, block_order):
    retiring = N_INST - 1
    first_retired = retiring * SLOTS
    block_count = N_CTX * N_CTX
    block_len = CACHE_LENGTH // block_count
    feature_rows = KEY_HEADS * HEAD_SIZE
    query_group = QUERY_HEADS // KEY_HEADS
    stored = cache[:, first_retired:].reshape(2, SLOTS, block_count, block_len, feature_rows)
    holder = jnp.zeros((block_count,), jnp.int32).at[block_order].set(jnp.arange(block_count, dtype=jnp.int32))
    logical = jnp.take(stored, holder, axis=2).reshape(2, SLOTS, CACHE_LENGTH, feature_rows)
    slot_ids = jnp.arange(GLOBAL_SLOTS, dtype=jnp.int32)
    instance_of = slot_ids // SLOTS
    within = slot_ids % SLOTS
    request_ids = jnp.arange(SLOTS, dtype=jnp.int32)
    match = (dest_inst[None, :] == instance_of[:, None]) & (dest_slot[None, :] == within[:, None])
    taken = jnp.any(match, axis=1)
    request = lax.optimization_barrier(jnp.sum(match.astype(jnp.int32) * request_ids[None, :], axis=1)).astype(jnp.int32)
    staying = jnp.logical_not(taken) & (instance_of < retiring)
    moved_len = lengths[first_retired + request]
    new_len = jnp.where(taken, moved_len, jnp.where(staying, lengths, 0)).astype(jnp.int32)
    active = new_len > 0
    moved_hidden = jnp.take(hidden, first_retired + request, axis=1)
    x_rows = jnp.where(taken[None, :, None], moved_hidden, hidden)
    flat = x_rows.reshape(TOKEN_STEPS * GLOBAL_SLOTS, MODEL_WIDTH).astype(jnp.float32)
    mean = lax.optimization_barrier(jnp.mean(flat, axis=1))
    mean_sq = lax.optimization_barrier(jnp.mean(flat * flat, axis=1))
    scale_rows = lax.rsqrt(mean_sq - mean * mean + NORM_EPSILON)
    scaled = (flat * norm_gain.astype(jnp.float32)).astype(jnp.bfloat16)

    def project(weight):
        gained = jnp.dot(norm_gain, weight, preferred_element_type=jnp.float32)
        product = jnp.dot(scaled, weight, preferred_element_type=jnp.float32)
        return scale_rows[:, None] * (product - mean[:, None] * gained[None, :])
    query = project(w_query)
    key_entries = project(key_value_weight[0])
    value_rows = project(key_value_weight[1])
    token_positions = new_len[None, :] + jnp.arange(TOKEN_STEPS, dtype=jnp.int32)[:, None]
    query_rot = apply_rotary(query.reshape(TOKEN_STEPS, GLOBAL_SLOTS, QUERY_HEADS, HEAD_SIZE), token_positions).astype(jnp.bfloat16)
    rotated_key = apply_rotary(key_entries.reshape(TOKEN_STEPS, GLOBAL_SLOTS, KEY_HEADS, HEAD_SIZE), token_positions).astype(jnp.bfloat16)
    value_new = value_rows.reshape(TOKEN_STEPS, GLOBAL_SLOTS, feature_rows).astype(jnp.bfloat16)
    entries = jnp.stack([rotated_key.reshape(TOKEN_STEPS, GLOBAL_SLOTS, feature_rows), value_new])
    grid = jnp.arange(CACHE_LENGTH, dtype=jnp.int32)

    def per_slot(slot):
        own = lax.dynamic_index_in_dim(cache, slot, 1, keepdims=False)
        arrived = lax.dynamic_index_in_dim(logical, request[slot], 1, keepdims=False)
        length = new_len[slot]
        live = active[slot]
        current_token = jnp.where(taken[slot], arrived, own)
        current_token = jnp.where(((grid < length) & live)[None, :, None], current_token, jnp.zeros_like(current_token))
        slot_entries = lax.dynamic_index_in_dim(entries, slot, 2, keepdims=False)
        for step in range(TOKEN_STEPS):
            hit = (grid == length + step) & live
            current_token = jnp.where(hit[None, :, None], slot_entries[:, step][:, None, :], current_token)
        cached_keys = current_token[0].reshape(CACHE_LENGTH, KEY_HEADS, HEAD_SIZE).astype(jnp.float32)
        cached_values = current_token[1].reshape(CACHE_LENGTH, KEY_HEADS, HEAD_SIZE).astype(jnp.float32)
        query_per_slot = lax.dynamic_index_in_dim(query_rot, slot, 1, keepdims=False)
        query_per_slot = query_per_slot.reshape(TOKEN_STEPS, KEY_HEADS, query_group, HEAD_SIZE).astype(jnp.float32)
        scores = jnp.einsum('tgjd,pgd->tgjp', query_per_slot, cached_keys) * HEAD_SIZE ** (-0.5)
        limit = length + jnp.arange(TOKEN_STEPS, dtype=jnp.int32)
        visible = ((grid[None, :] <= limit[:, None]) & live)[:, None, None, :]
        masked = jnp.where(visible, scores, MASKED_SCORE)
        peak = lax.optimization_barrier(jnp.max(masked, axis=-1, keepdims=True))
        weights = jnp.where(visible, jnp.exp(masked - peak), 0.0)
        total = lax.optimization_barrier(jnp.sum(weights, axis=-1))
        rounded = lax.optimization_barrier(weights.astype(jnp.bfloat16)).astype(jnp.float32)
        mixed = jnp.einsum('tgjp,pgd->tgjd', rounded, cached_values)
        attended = (mixed / jnp.where(total > 0, total, 1.0)[..., None]).astype(jnp.bfloat16)
        return (current_token, attended.reshape(TOKEN_STEPS, QUERY_HEADS * HEAD_SIZE))
    caches, attended = lax.map(per_slot, slot_ids)
    new_cache = jnp.moveaxis(caches, 0, 1)
    rows = jnp.transpose(attended, (1, 0, 2)).reshape(TOKEN_STEPS * GLOBAL_SLOTS, QUERY_HEADS * HEAD_SIZE)
    attn_out = jnp.dot(rows, w_out, preferred_element_type=jnp.float32).astype(jnp.bfloat16)
    return (new_cache, attn_out.reshape(TOKEN_STEPS, GLOBAL_SLOTS, MODEL_WIDTH))
```

```python
import functools

import jax
import jax.numpy as jnp
from jax import lax
from jax.experimental import pallas as pl
from jax.experimental.pallas import tpu as pltpu
from jax.sharding import PartitionSpec as P

MODEL_WIDTH = 6144
HEAD_SIZE = 128
ROPE_BASE = 500000.0
NORM_EPSILON = 1e-05
MASKED_SCORE = -1e30

INST = 4
CTX = 16
SLOTS = 8
STEPS = 3
MOVED = 3
BLOCK = 32
RANGE = 512
FEATURES = 512
HALF_ROWS = 48
STAT_ROW = 40
CHUNKS = 4
BF16 = jnp.bfloat16
F32 = jnp.float32
I32 = jnp.int32

NEW_LEN, STAYS, REQUEST = 0, 8, 16
VALID, SLOT, LENGTH, COUNT = 24, 28, 32, 36
STORED, LOGICAL = 48, 64
NEED = 80
SOURCE, TARGET = 128, 256
PLAN_SIZE = 384
LIST = 64

VMEM = pl.BlockSpec(memory_space=pltpu.VMEM)
SMEM = pl.BlockSpec(memory_space=pltpu.SMEM)
ANY = pl.BlockSpec(memory_space=pl.ANY)


def params(**more):
    return pltpu.CompilerParams(vmem_limit_bytes=60 * 1024 * 1024, **more)


def plan_kernel(ids, lengths, dest_inst, dest_slot, order, plan):
    inst = ids[0]
    ctx = ids[1]

    def clear(p, carry):
        plan[SOURCE + p] = 0
        plan[TARGET + p] = -1
        return carry

    lax.fori_loop(0, 2 * LIST, clear, 0)
    for s in range(SLOTS):
        own = jnp.where(inst == INST - 1, 0, lengths[inst * SLOTS + s])
        plan[NEW_LEN + s] = own
        plan[STAYS + s] = jnp.where(own > 0, 1, 0)
        plan[REQUEST + s] = -1
    for j in range(4):
        plan[VALID + j] = 0
        plan[SLOT + j] = 0
        plan[LENGTH + j] = 0
        plan[COUNT + j] = 0
    for b in range(CTX):
        q = order[ctx * CTX + b]
        plan[STORED + lax.shift_right_logical(q, 4)] = b
        plan[LOGICAL + lax.shift_right_logical(q, 4)] = q

    counts = []
    total = [jnp.int32(0)] * 3
    for r in range(SLOTS):
        long = lengths[(INST - 1) * SLOTS + r]
        count = lax.shift_right_logical(long + STEPS + RANGE - 1, 9)
        counts.append(count)
        to = dest_inst[r]
        total = [total[i] + jnp.where(to == i, count, 0) for i in range(3)]
    split = jnp.clip(lax.shift_right_arithmetic(total[2] + total[1] - total[0] + 1, 1), 0, total[1])
    rest = total[1] - split
    plan[NEED] = jnp.maximum(split + total[0], rest + total[2])
    plan[NEED + 1] = jnp.maximum(split, rest)

    done = [jnp.int32(0)] * 3
    rank = [jnp.int32(0)] * 3
    for r in range(SLOTS):
        to = dest_inst[r]
        count = counts[r]
        base = jnp.where(to == 0, done[0], jnp.where(to == 1, done[1], done[2]))
        place = jnp.where(to == 0, rank[0], jnp.where(to == 1, rank[1], rank[2]))

        def put(c, carry, r=r, to=to, base=base, place=place):
            e = base + c
            by_zero = jnp.logical_or(to == 0, jnp.logical_and(to == 1, e < split))
            p = jnp.where(
                to == 0,
                split + e,
                jnp.where(to == 2, LIST + rest + e, jnp.where(e < split, e, LIST + e - split)),
            )
            plan[SOURCE + p] = r * CTX + c
            plan[TARGET + p] = to * 64 + place * CTX + c
            return carry

        lax.fori_loop(0, count, put, 0)

        @pl.when(to == inst)
        def _(r=r, place=place, count=count):
            long = lengths[(INST - 1) * SLOTS + r]
            slot = dest_slot[r]
            plan[NEW_LEN + slot] = long
            plan[STAYS + slot] = 0
            plan[REQUEST + slot] = r
            plan[VALID + place] = jnp.where(long > 0, 1, 0)
            plan[SLOT + place] = slot
            plan[LENGTH + place] = long
            plan[COUNT + place] = count

        done = [done[i] + jnp.where(to == i, count, 0) for i in range(3)]
        rank = [rank[i] + jnp.where(to == i, 1, 0) for i in range(3)]


def make_plan(ids, lengths, dest_inst, dest_slot, order):
    return pl.pallas_call(
        plan_kernel,
        out_shape=jax.ShapeDtypeStruct((PLAN_SIZE,), I32),
        in_specs=[SMEM] * 5,
        out_specs=SMEM,
        name="plan",
    )(ids, lengths, dest_inst, dest_slot, order)


def pack_kernel(chunk, items, ids, plan, cache, up, down, sem):
    @pl.when(ids[0] == INST - 1)
    def _():
        for way, out in enumerate((up, down)):

            def send(i, carry, way=way, out=out):
                code = plan[SOURCE + way * LIST + chunk * items + i]
                r = lax.shift_right_logical(code, 4)
                stored = plan[STORED + lax.bitwise_and(code, 15)]
                rows = pl.ds(pl.multiple_of(stored * BLOCK, BLOCK), BLOCK)
                pltpu.make_async_copy(cache.at[:, r, rows, :], out.at[i], sem.at[way]).start()
                return carry

            lax.fori_loop(0, items, send, 0)
        for way, out in enumerate((up, down)):
            pltpu.make_async_copy(out, out, sem.at[way]).wait()


def pack(chunk, items, ids, plan, cache):
    shape = jax.ShapeDtypeStruct((items, 2, BLOCK, FEATURES), BF16)
    return pl.pallas_call(
        functools.partial(pack_kernel, chunk, items),
        out_shape=[shape, shape],
        in_specs=[SMEM, SMEM, ANY],
        out_specs=[VMEM, VMEM],
        scratch_shapes=[pltpu.SemaphoreType.DMA((2,))],
        cost_estimate=pl.CostEstimate(
            flops=0, bytes_accessed=8 * items * BLOCK * FEATURES * 2, transcendentals=0
        ),
        compiler_params=params(),
        name="pack",
    )(ids, plan, cache)


def to_lanes(column, rows):
    shape = (rows, 128)
    same = lax.broadcasted_iota(I32, shape, 0) == lax.broadcasted_iota(I32, shape, 1)
    return jnp.sum(jnp.where(same, column, 0.0), axis=0, keepdims=True)


def to_rows(lanes, rows):
    shape = (rows, 128)
    same = lax.broadcasted_iota(I32, shape, 0) == lax.broadcasted_iota(I32, shape, 1)
    return jnp.sum(jnp.where(same, lanes, 0.0), axis=1, keepdims=True)


def project_kernel(plan, hidden, by0, by1, by2, gain, w_query, w_kv, out, lhs, stats):
    step = pl.program_id(0)

    @pl.when(step == 0)
    def _():
        row = lax.broadcasted_iota(I32, (SLOTS, 1), 0)
        request = jnp.full((SLOTS, 1), -1, I32)
        for s in range(SLOTS):
            request = jnp.where(row == s, plan[REQUEST + s], request)
        scale = gain[...].astype(F32)
        sums = []
        squares = []
        for t in range(STEPS):
            x = hidden[t].astype(F32)
            moved = by0[t].astype(F32) + by1[t].astype(F32) + by2[t].astype(F32)
            for r in range(SLOTS):
                x = jnp.where(request == r, moved[r : r + 1, :], x)
            sums.append(jnp.sum(x, axis=1, keepdims=True))
            squares.append(jnp.sum(x * x, axis=1, keepdims=True))
            lhs[t * SLOTS : (t + 1) * SLOTS, :] = x * scale
        lhs[24:32, :] = jnp.where(row == 0, scale, 0.0)
        sum_lanes = to_lanes(jnp.concatenate(sums, axis=0), 24)
        square_lanes = to_lanes(jnp.concatenate(squares, axis=0), 24)
        stats[...] = jnp.where(row == 1, sum_lanes, jnp.where(row == 2, square_lanes, 0.0))

    left = lhs[...].astype(BF16)
    tail = stats[...]
    row = lax.broadcasted_iota(I32, (SLOTS, 256), 0)
    wide = jnp.concatenate([tail, tail], axis=1)

    def store(o, weight):
        got = jnp.dot(left, weight, preferred_element_type=F32)
        out[o, 0:24, :] = got[0:24]
        out[o, 24:32, :] = jnp.where(row == 0, got[24:32], wide)

    @pl.when(step < 3)
    def _():
        for o in range(4):
            store(o, w_query[:, o * 256 : (o + 1) * 256])

    @pl.when(step == 3)
    def _():
        for o in range(4):
            store(o, w_kv[o // 2, :, (o % 2) * 256 : (o % 2 + 1) * 256])


def project(plan, hidden, by, gain, w_query, w_kv):
    def whole(*shape):
        return pl.BlockSpec(shape, lambda i: (0,) * len(shape))

    small = whole(3, 8, 384)
    return pl.pallas_call(
        project_kernel,
        out_shape=jax.ShapeDtypeStruct((CTX, 32, 256), F32),
        grid=(4,),
        in_specs=[SMEM, small, small, small, small, whole(1, 384)]
        + [
            pl.BlockSpec((384, 1024), lambda i: (0, jnp.minimum(i, 2))),
            whole(2, 384, 512),
        ],
        out_specs=pl.BlockSpec((4, 32, 256), lambda i: (i, 0, 0)),
        scratch_shapes=[pltpu.VMEM((32, 384), F32), pltpu.VMEM((8, 128), F32)],
        cost_estimate=pl.CostEstimate(
            flops=2 * 32 * 384 * 4096, bytes_accessed=384 * 4096 * 2, transcendentals=0
        ),
        compiler_params=params(),
        name="project",
    )(plan, hidden, *by, gain, w_query, w_kv)


def rotate_kernel(parts, cosine, sine, out):
    total = parts[0]
    for d in range(1, CTX):
        total = total + parts[d]
    row = total[24:32]
    mean = to_rows(row[1:2, :128], 24) / MODEL_WIDTH
    square = to_rows(row[2:3, :128], 24) / MODEL_WIDTH
    scale = lax.rsqrt(square - mean * mean + NORM_EPSILON)
    value = scale * (total[0:24] - mean * row[0:1])
    for h in range(2):
        part = value[:, h * 128 : (h + 1) * 128]
        turned = part * cosine[...] + pltpu.roll(part, 64, 1) * sine[...]
        turned = turned.astype(BF16)
        for d in range(CTX):
            out[d, h] = turned


def rotate(parts, cosine, sine):
    return pl.pallas_call(
        rotate_kernel,
        out_shape=jax.ShapeDtypeStruct((CTX, 2, 24, 128), BF16),
        in_specs=[VMEM] * 3,
        out_specs=VMEM,
        compiler_params=params(),
        name="rotate",
    )(parts, cosine, sine)


def attend(keys, values, query, position, length):
    rows = 2 * HALF_ROWS
    row = lax.broadcasted_iota(I32, (rows, 128), 0)
    high = row >= HALF_ROWS
    within = jnp.where(high, row - HALF_ROWS, row)
    group = jnp.where(high, 2, 0) + jnp.where(within >= 18, 1, 0)
    q = query.astype(F32)
    wide = jnp.concatenate([jnp.where(group == g, q, 0.0) for g in range(4)], axis=1).astype(BF16)
    score = lax.dot_general(
        wide, keys, (((1,), (1,)), ((), ())), preferred_element_type=F32
    ) * (HEAD_SIZE ** -0.5)
    line = lax.broadcasted_iota(I32, (rows, 1), 0)
    line = jnp.where(line >= HALF_ROWS, line - HALF_ROWS, line)
    visible = position <= length + lax.rem(line, STEPS)
    masked = jnp.where(visible, score, MASKED_SCORE)
    peak = jnp.max(masked, axis=1, keepdims=True)
    weight = jnp.where(visible, jnp.exp(masked - peak), 0.0)
    total = jnp.sum(weight, axis=1, keepdims=True)
    mixed = jnp.dot(weight.astype(BF16), values, preferred_element_type=F32)
    out = jnp.zeros((rows, 128), F32)
    for g in range(4):
        out = out + jnp.where(group == g, mixed[:, g * 128 : (g + 1) * 128], 0.0)
    return [
        message(
            out[h * HALF_ROWS : (h + 1) * HALF_ROWS],
            peak[h * HALF_ROWS : (h + 1) * HALF_ROWS],
            total[h * HALF_ROWS : (h + 1) * HALF_ROWS],
        )
        for h in range(2)
    ]


def message(out, peak, total):
    peak = to_lanes(peak, HALF_ROWS)
    total = to_lanes(total, HALF_ROWS)
    parts = []
    for value, count in ((peak, 3), (total, 2)):
        for _ in range(count):
            part = value.astype(BF16).astype(F32)
            parts.append(part)
            value = value - part
    row = lax.broadcasted_iota(I32, (HALF_ROWS, 128), 0)
    for i, part in enumerate(parts):
        out = jnp.where(row == STAT_ROW + i, part, out)
    return out.astype(BF16)


def blank_message():
    row = lax.broadcasted_iota(I32, (HALF_ROWS, 128), 0)
    return jnp.where(row == STAT_ROW, MASKED_SCORE, 0.0).astype(BF16)


def stay_kernel(ids, plan, cache, query, entries, new_cache, sums):
    s = pl.program_id(0)
    base = ids[1] * RANGE
    length = plan[NEW_LEN + s]
    stays = plan[STAYS + s] > 0
    some = jnp.logical_and(stays, base < length + STEPS)
    full = jnp.logical_and(some, base + RANGE <= length)

    @pl.when(full)
    def _():
        new_cache[...] = cache[...]

    @pl.when(jnp.logical_and(some, jnp.logical_not(full)))
    def _():
        at = base + lax.broadcasted_iota(I32, (RANGE, 1), 0)
        for kv in range(2):
            block = jnp.where(at < length, cache[kv, 0], jnp.zeros((), BF16))
            for t in range(STEPS):
                block = jnp.where(at == length + t, entries[0, kv, t : t + 1, :], block)
            new_cache[kv, 0] = block

    @pl.when(some)
    def _():
        position = base + lax.broadcasted_iota(I32, (1, RANGE), 1)
        halves = attend(new_cache[0, 0], new_cache[1, 0], query[0], position, length)
        for h in range(2):
            sums[0, h] = halves[h]

    @pl.when(jnp.logical_not(some))
    def _():
        new_cache[...] = jnp.zeros_like(new_cache)
        for h in range(2):
            sums[0, h] = blank_message()


def stay(ids, plan, cache, query, entries):
    return pl.pallas_call(
        stay_kernel,
        out_shape=[
            jax.ShapeDtypeStruct(cache.shape, BF16),
            jax.ShapeDtypeStruct((SLOTS, 2, HALF_ROWS, 128), BF16),
        ],
        grid=(SLOTS,),
        in_specs=[
            SMEM,
            SMEM,
            pl.BlockSpec((2, 1, RANGE, FEATURES), lambda s: (0, s, 0, 0)),
            pl.BlockSpec((1, 2 * HALF_ROWS, 128), lambda s: (s, 0, 0)),
            pl.BlockSpec((1, 2, 8, FEATURES), lambda s: (s, 0, 0, 0)),
        ],
        out_specs=[
            pl.BlockSpec((2, 1, RANGE, FEATURES), lambda s: (0, s, 0, 0)),
            pl.BlockSpec((1, 2, HALF_ROWS, 128), lambda s: (s, 0, 0, 0)),
        ],
        cost_estimate=pl.CostEstimate(
            flops=0, bytes_accessed=32 * 1024 * 1024, transcendentals=0
        ),
        compiler_params=params(),
        name="stay",
    )(ids, plan, cache, query, entries)


def moved_kernel(items, ids, plan, query, entries, sums, *refs):
    count = 4 * CHUNKS - 2
    arrived, (held, new_sums, sem) = refs[:count], refs[count:]
    straight = (arrived[:CHUNKS], arrived[CHUNKS : 2 * CHUNKS])
    onward = (arrived[2 * CHUNKS : 3 * CHUNKS - 1], arrived[3 * CHUNKS - 1 :])
    inst = ids[0]

    def fetch(way, chunk, ref, target):
        def one(i, carry):
            code = plan[TARGET + way * LIST + chunk * items + i]
            inside = lax.bitwise_and(code, 63)

            @pl.when(lax.shift_right_arithmetic(code, 6) == target)
            def _():
                place = lax.shift_right_logical(inside, 4)
                c = lax.bitwise_and(inside, 15)
                pltpu.make_async_copy(ref.at[i], held.at[c, place], sem).start()

            return carry

        lax.fori_loop(0, items, one, 0)

    for way, target in ((0, 0), (1, 2)):

        @pl.when(inst == target)
        def _(way=way, target=target):
            for chunk in range(CHUNKS):
                fetch(way, chunk, straight[way][chunk], target)

    @pl.when(inst == 1)
    def _():
        for way in range(2):
            for chunk in range(CHUNKS - 1):
                fetch(way, chunk, onward[way][chunk], 1)

    new_sums[...] = sums[...]

    @pl.when(inst < INST - 1)
    def _():
        for j in range(MOVED):

            def fill(c, carry, j=j):
                pltpu.make_async_copy(arrived[0].at[0], held.at[c, j], sem).start()
                return carry

            lax.fori_loop(plan[COUNT + j], CTX, fill, 0)
        pltpu.make_async_copy(held, held, sem).wait()

    for j in range(MOVED):

        @pl.when(plan[VALID + j] > 0)
        def _(j=j):
            slot = plan[SLOT + j]
            length = plan[LENGTH + j]
            lane = lax.broadcasted_iota(I32, (1, RANGE), 1)
            position = jnp.zeros((1, RANGE), I32)
            at = lax.broadcasted_iota(I32, (BLOCK, 1), 0)
            for c in range(CTX):
                start = plan[LOGICAL + c] * BLOCK
                position = jnp.where(
                    lax.shift_right_logical(lane, 5) == c, start + lane - c * BLOCK, position
                )

                @pl.when(start + BLOCK > length)
                def _(c=c, start=start):
                    for kv in range(2):
                        block = jnp.where(start + at < length, held[c, j, kv], jnp.zeros((), BF16))
                        new = entries[slot, kv]
                        for t in range(STEPS):
                            block = jnp.where(start + at == length + t, new[t : t + 1, :], block)
                        held[c, j, kv] = block

            keys = held[:, j, 0].reshape(RANGE, FEATURES)
            values = held[:, j, 1].reshape(RANGE, FEATURES)
            halves = attend(keys, values, query[slot], position, length)
            for h in range(2):
                new_sums[slot, h] = halves[h]


def attend_moved(items, ids, plan, query, entries, sums, arrived):
    return pl.pallas_call(
        functools.partial(moved_kernel, items),
        out_shape=[
            jax.ShapeDtypeStruct((CTX, MOVED, 2, BLOCK, FEATURES), BF16),
            jax.ShapeDtypeStruct(sums.shape, BF16),
        ],
        in_specs=[SMEM, SMEM, VMEM, VMEM, VMEM] + [ANY] * len(arrived),
        out_specs=[VMEM, VMEM],
        scratch_shapes=[pltpu.SemaphoreType.DMA(())],
        cost_estimate=pl.CostEstimate(
            flops=0, bytes_accessed=16 * 1024 * 1024, transcendentals=0
        ),
        compiler_params=params(),
        name="moved",
    )(ids, plan, query, entries, sums, *arrived)


def merge_kernel(parts, out):
    blocks = [parts[d].astype(F32) for d in range(CTX)]
    peaks = []
    totals = []
    for block in blocks:
        stat = block[STAT_ROW : STAT_ROW + 8]
        peaks.append(stat[0:1] + stat[1:2] + stat[2:3])
        totals.append(stat[3:4] + stat[4:5])
    peak = functools.reduce(jnp.maximum, peaks)
    factors = [jnp.exp(p - peak) for p in peaks]
    total = functools.reduce(jnp.add, [f * t for f, t in zip(factors, totals)])
    under = to_rows(jnp.where(total > 0, total, 1.0), HALF_ROWS)
    mixed = functools.reduce(
        jnp.add, [to_rows(f, HALF_ROWS) * b for f, b in zip(factors, blocks)]
    )
    attended = (mixed / under).astype(BF16)
    for d in range(CTX):
        out[d] = attended


def merge(parts):
    return pl.pallas_call(
        merge_kernel,
        out_shape=jax.ShapeDtypeStruct(parts.shape, BF16),
        in_specs=[VMEM],
        out_specs=VMEM,
        compiler_params=params(),
        name="merge",
    )(parts)


def place_kernel(plan, within, received, cache, new_cache, held, read_sem, write_sem):
    for j in range(MOVED):

        @pl.when(plan[VALID + j] > 0)
        def _(j=j):
            def one(d, carry):
                rows = pl.ds(pl.multiple_of(within[d] * BLOCK, BLOCK), BLOCK)
                pltpu.make_async_copy(
                    received.at[d, j], held.at[j, :, rows, :], read_sem.at[j]
                ).start()
                return carry

            lax.fori_loop(0, CTX, one, 0)

    for j in range(MOVED):

        @pl.when(plan[VALID + j] > 0)
        def _(j=j):
            pltpu.make_async_copy(held.at[j], held.at[j], read_sem.at[j]).wait()
            pltpu.make_async_copy(
                held.at[j], new_cache.at[:, plan[SLOT + j]], write_sem.at[j]
            ).start()

    for j in range(MOVED):

        @pl.when(plan[VALID + j] > 0)
        def _(j=j):
            pltpu.make_async_copy(
                held.at[j], new_cache.at[:, plan[SLOT + j]], write_sem.at[j]
            ).wait()


def place(plan, within, received, cache):
    return pl.pallas_call(
        place_kernel,
        out_shape=jax.ShapeDtypeStruct(cache.shape, BF16),
        in_specs=[SMEM, SMEM, ANY, ANY],
        out_specs=ANY,
        scratch_shapes=[
            pltpu.VMEM((MOVED, 2, RANGE, FEATURES), BF16),
            pltpu.SemaphoreType.DMA((MOVED,)),
            pltpu.SemaphoreType.DMA((MOVED,)),
        ],
        input_output_aliases={3: 0},
        compiler_params=params(),
        name="place",
    )(plan, within, received, cache)


def swap(x):
    return lax.all_to_all(x, "ctx", split_axis=0, concat_axis=0, tiled=True)


def after(*values):
    return lax.optimization_barrier(values)


def shards(
    cache,
    hidden,
    norm_gain,
    w_query,
    key_value_weight,
    w_out,
    lengths,
    dest_inst,
    dest_slot,
    block_order,
):
    instance = lax.axis_index("inst")
    context = lax.axis_index("ctx")
    head = lax.axis_index("head")
    ids = jnp.stack([instance, context]).astype(I32)
    by = [lax.ppermute(hidden, "inst", [(INST - 1, i)]) for i in range(INST - 1)]
    plan = make_plan(ids, lengths, dest_inst, dest_slot, block_order)
    by, plan = after(by, plan)
    layout = block_order.reshape(CTX, CTX)
    within = jnp.sum(jnp.where(layout // CTX == context, layout % CTX, 0), axis=1)
    new_len = plan[NEW_LEN : NEW_LEN + SLOTS]
    token = new_len[None, :] + jnp.arange(STEPS, dtype=I32)[:, None]
    half = HEAD_SIZE // 2
    frequency = ROPE_BASE ** (-jnp.arange(half, dtype=F32) * 2.0 / HEAD_SIZE)
    angles = token.astype(F32).reshape(24, 1) * frequency
    is_value = context >= 14
    cosine = jnp.where(is_value, 1.0, jnp.cos(angles))
    sine = jnp.where(is_value, 0.0, jnp.sin(angles))
    cosine = jnp.concatenate([cosine, cosine], axis=1)
    sine = jnp.concatenate([-sine, sine], axis=1)

    items = LIST // CHUNKS
    up, down, up_on, down_on = [], [], [], []

    def send(chunk, plan):
        one, two = pack(chunk, items, ids, plan, cache)
        up.append(lax.ppermute(one, "inst", [(INST - 1, 0)]))
        down.append(lax.ppermute(two, "inst", [(INST - 1, 2)]))
        if chunk < CHUNKS - 1:
            up_on.append(lax.ppermute(up[-1], "inst", [(0, 1)]))
            down_on.append(lax.ppermute(down[-1], "inst", [(2, 1)]))
        return one

    send(0, plan)
    packed = send(1, plan)
    hidden, cosine, sine, within, packed = after(hidden, cosine, sine, within, packed)
    parts = swap(project(plan, hidden, by, norm_gain[None], w_query, key_value_weight))
    parts, plan_2 = after(parts, plan)
    packed = send(2, plan_2)
    parts, packed = after(parts, packed)
    turned = swap(rotate(parts, cosine, sine))
    turned, plan_3 = after(turned, plan)
    packed = send(3, plan_3)
    turned, packed = after(turned, packed)
    turned = turned.reshape(32, STEPS, SLOTS, HEAD_SIZE)
    query = turned[:24].reshape(2, 12, STEPS, SLOTS, HEAD_SIZE).transpose(3, 0, 1, 2, 4)
    query = query.reshape(SLOTS, 2, 36, HEAD_SIZE)
    query = jnp.pad(query, ((0, 0), (0, 0), (0, HALF_ROWS - 36), (0, 0)))
    query = query.reshape(SLOTS, 2 * HALF_ROWS, HEAD_SIZE)
    entries = turned[24:].reshape(2, 4, STEPS, SLOTS, HEAD_SIZE).transpose(3, 0, 2, 1, 4)
    entries = entries.reshape(SLOTS, 2, STEPS, FEATURES)
    entries = jnp.pad(entries, ((0, 0), (0, 0), (0, 8 - STEPS), (0, 0)))
    query, entries, up_on[0], down_on[0] = after(query, entries, up_on[0], down_on[0])

    new_cache, sums = stay(ids, plan, cache, query, entries)
    held, sums = attend_moved(
        items, ids, plan, query, entries, sums, up + down + up_on + down_on
    )
    received = swap(held)
    received, sums = after(received, sums)
    attended = swap(merge(swap(sums.reshape(CTX, HALF_ROWS, HEAD_SIZE))))
    new_cache = place(plan, within, received, new_cache)

    attended = attended[:, :36].reshape(SLOTS, 2, 12, STEPS, HEAD_SIZE)
    attended = attended.transpose(3, 0, 1, 2, 4).reshape(24, 24 * HEAD_SIZE)
    projected = jnp.dot(attended, w_out, preferred_element_type=F32)
    mine, other = projected[:, :192], projected[:, 192:]
    first = head == 0
    keep = jnp.where(first, mine, other)
    send = jnp.where(first, other, mine).astype(BF16)
    got = lax.ppermute(send, "head", [(0, 1), (1, 0)])
    attn_out = (keep + got.astype(F32)).astype(BF16)
    return new_cache, attn_out.reshape(STEPS, SLOTS, 192)


def solution(mesh):
    placed = (
        P(None, "inst", "ctx", "head"),
        P(None, "inst", "ctx"),
        P("ctx"),
        P("ctx", "head"),
        P(None, "ctx", "head"),
        P("head", "ctx"),
        P(),
        P(),
        P(),
        P(),
    )
    return jax.shard_map(
        shards,
        mesh=mesh,
        in_specs=placed,
        out_specs=(P(None, "inst", "ctx", "head"), P(None, "inst", ("ctx", "head"))),
        check_vma=False,
    )
```

```python
import functools

import jax
import jax.numpy as jnp
from jax import lax
from jax.experimental import pallas as pl
from jax.experimental.pallas import tpu as pltpu
from jax.sharding import PartitionSpec as P

MODEL_WIDTH = 6144
HEAD_SIZE = 128
ROPE_BASE = 500000.0
NORM_EPSILON = 1e-05
MASKED_SCORE = -1e30

INST = 4
CTX = 16
SLOTS = 8
STEPS = 3
MOVED = 3
BLOCK = 32
RANGE = 512
FEATURES = 512
HALF_ROWS = 48
STAT_ROW = 40
CHUNKS = 2
ITEMS = (12, 15, 18, 21, 24, 28, 33)
BF16 = jnp.bfloat16
F32 = jnp.float32
I32 = jnp.int32

NEW_LEN, STAYS, REQUEST = 0, 8, 16
VALID, SLOT, LENGTH, COUNT = 24, 28, 32, 36
STORED, LOGICAL, WITHIN = 48, 64, 80
NEED = 96
SOURCE, TARGET = 128, 272
PLAN_SIZE = 416
LIST = 72

VMEM = pl.BlockSpec(memory_space=pltpu.VMEM)
SMEM = pl.BlockSpec(memory_space=pltpu.SMEM)
ANY = pl.BlockSpec(memory_space=pl.ANY)
HBM = pl.BlockSpec(memory_space=pltpu.HBM)


def params(mib):
    return pltpu.CompilerParams(vmem_limit_bytes=mib * 1024 * 1024)


def plan_kernel(lengths, dest_inst, dest_slot, order, plan):
    inst = lax.axis_index("inst")
    ctx = lax.axis_index("ctx")

    def clear(p, carry):
        plan[SOURCE + p] = 0
        plan[TARGET + p] = -1
        return carry

    lax.fori_loop(0, 2 * LIST, clear, 0)
    for s in range(SLOTS):
        own = jnp.where(inst == INST - 1, 0, lengths[inst * SLOTS + s])
        plan[NEW_LEN + s] = own
        plan[STAYS + s] = jnp.where(own > 0, 1, 0)
        plan[REQUEST + s] = -1
    for j in range(4):
        plan[VALID + j] = 0
        plan[SLOT + j] = 0
        plan[LENGTH + j] = 0
        plan[COUNT + j] = 0
    for b in range(CTX):
        q = order[ctx * CTX + b]
        plan[STORED + lax.shift_right_logical(q, 4)] = b
        plan[LOGICAL + lax.shift_right_logical(q, 4)] = q

    def search(d, carry):
        found = jnp.int32(0)
        for b in range(CTX):
            q = order[d * CTX + b]
            mine = lax.shift_right_logical(q, 4) == ctx
            found = jnp.where(mine, lax.bitwise_and(q, CTX - 1), found)
        plan[WITHIN + d] = found
        return carry

    lax.fori_loop(0, CTX, search, 0)

    counts = []
    total = [jnp.int32(0)] * 3
    for r in range(SLOTS):
        long = lengths[(INST - 1) * SLOTS + r]
        count = lax.shift_right_logical(long + STEPS + RANGE - 1, 9)
        counts.append(count)
        to = dest_inst[r]
        total = [total[i] + jnp.where(to == i, count, 0) for i in range(3)]
    def weigh(part, best):
        rest = total[1] - part
        cost = jnp.maximum(
            lax.shift_right_logical(jnp.maximum(part + total[0], rest + total[2]) + 1, 1),
            jnp.maximum(part, rest),
        )
        better = cost < best[0]
        return jnp.where(better, cost, best[0]), jnp.where(better, part, best[1])

    least, split = lax.fori_loop(0, total[1] + 1, weigh, (jnp.int32(1000), jnp.int32(0)))
    rest = total[1] - split
    size = jnp.int32(0)
    for items in ITEMS[:-1]:
        size = size + jnp.where(least > items, 1, 0)
    plan[NEED] = size

    done = [jnp.int32(0)] * 3
    rank = [jnp.int32(0)] * 3
    for r in range(SLOTS):
        to = dest_inst[r]
        count = counts[r]
        base = jnp.where(to == 0, done[0], jnp.where(to == 1, done[1], done[2]))
        place = jnp.where(to == 0, rank[0], jnp.where(to == 1, rank[1], rank[2]))

        def put(c, carry, r=r, to=to, base=base, place=place):
            e = base + c
            by_zero = jnp.logical_or(to == 0, jnp.logical_and(to == 1, e < split))
            p = jnp.where(
                to == 0,
                split + e,
                jnp.where(to == 2, LIST + rest + e, jnp.where(e < split, e, LIST + e - split)),
            )
            plan[SOURCE + p] = r * CTX + c
            plan[TARGET + p] = to * 64 + place * CTX + c
            return carry

        lax.fori_loop(0, count, put, 0)

        @pl.when(to == inst)
        def _(r=r, place=place, count=count):
            long = lengths[(INST - 1) * SLOTS + r]
            slot = dest_slot[r]
            plan[NEW_LEN + slot] = long
            plan[STAYS + slot] = 0
            plan[REQUEST + slot] = r
            plan[VALID + place] = jnp.where(long > 0, 1, 0)
            plan[SLOT + place] = slot
            plan[LENGTH + place] = long
            plan[COUNT + place] = count

        done = [done[i] + jnp.where(to == i, count, 0) for i in range(3)]
        rank = [rank[i] + jnp.where(to == i, 1, 0) for i in range(3)]


def make_plan(lengths, dest_inst, dest_slot, order):
    return pl.pallas_call(
        plan_kernel,
        out_shape=jax.ShapeDtypeStruct((PLAN_SIZE,), I32),
        in_specs=[SMEM] * 4,
        out_specs=SMEM,
        name="plan",
    )(lengths, dest_inst, dest_slot, order)


def pack_kernel(chunk, items, plan, cache, up, down, sem):
    @pl.when(lax.axis_index("inst") == INST - 1)
    def _():
        for way, out in enumerate((up, down)):

            def send(i, carry, way=way, out=out):
                code = plan[SOURCE + way * LIST + chunk * items + i]
                r = lax.shift_right_logical(code, 4)
                stored = plan[STORED + lax.bitwise_and(code, 15)]
                rows = pl.ds(pl.multiple_of(stored * BLOCK, BLOCK), BLOCK)
                pltpu.make_async_copy(cache.at[:, r, rows, :], out.at[i], sem.at[way]).start()
                return carry

            lax.fori_loop(0, items, send, 0)
        for way, out in enumerate((up, down)):
            pltpu.make_async_copy(out, out, sem.at[way]).wait()


def pack(chunk, items, plan, cache):
    shape = jax.ShapeDtypeStruct((items, 2, BLOCK, FEATURES), BF16)
    return pl.pallas_call(
        functools.partial(pack_kernel, chunk, items),
        out_shape=[shape, shape],
        in_specs=[SMEM, HBM],
        out_specs=[VMEM, VMEM],
        scratch_shapes=[pltpu.SemaphoreType.DMA((2,))],
        cost_estimate=pl.CostEstimate(
            flops=0, bytes_accessed=8 * items * BLOCK * FEATURES * 2, transcendentals=0
        ),
        compiler_params=params(16),
        name="pack",
    )(plan, cache)


def to_lanes(column, rows):
    shape = (rows, 128)
    same = lax.broadcasted_iota(I32, shape, 0) == lax.broadcasted_iota(I32, shape, 1)
    return jnp.sum(jnp.where(same, column, 0.0), axis=0, keepdims=True)


def to_rows(lanes, rows):
    shape = (rows, 128)
    same = lax.broadcasted_iota(I32, shape, 0) == lax.broadcasted_iota(I32, shape, 1)
    return jnp.sum(jnp.where(same, lanes, 0.0), axis=1, keepdims=True)


def project_kernel(plan, hidden, by0, by1, by2, gain, w_query, w_kv, out, lhs, stats):
    step = pl.program_id(0)

    @pl.when(step == 0)
    def _():
        row = lax.broadcasted_iota(I32, (SLOTS, 1), 0)
        request = jnp.full((SLOTS, 1), -1, I32)
        for s in range(SLOTS):
            request = jnp.where(row == s, plan[REQUEST + s], request)
        scale = gain[...].astype(F32)
        sums = []
        squares = []
        for t in range(STEPS):
            x = hidden[t].astype(F32)
            moved = by0[t].astype(F32) + by1[t].astype(F32) + by2[t].astype(F32)
            for r in range(SLOTS):
                x = jnp.where(request == r, moved[r : r + 1, :], x)
            sums.append(jnp.sum(x, axis=1, keepdims=True))
            squares.append(jnp.sum(x * x, axis=1, keepdims=True))
            lhs[t * SLOTS : (t + 1) * SLOTS, :] = x * scale
        lhs[24:32, :] = jnp.where(row == 0, scale, 0.0)
        sum_lanes = to_lanes(jnp.concatenate(sums, axis=0), 24)
        square_lanes = to_lanes(jnp.concatenate(squares, axis=0), 24)
        stats[...] = jnp.where(row == 1, sum_lanes, jnp.where(row == 2, square_lanes, 0.0))

    left = lhs[...].astype(BF16)
    tail = stats[...]
    row = lax.broadcasted_iota(I32, (SLOTS, 256), 0)
    wide = jnp.concatenate([tail, tail], axis=1)

    def store(o, weight):
        got = jnp.dot(left, weight, preferred_element_type=F32)
        out[o, 0:24, :] = got[0:24]
        out[o, 24:32, :] = jnp.where(row == 0, got[24:32], wide)

    @pl.when(step < 3)
    def _():
        for o in range(4):
            store(o, w_query[:, o * 256 : (o + 1) * 256])

    @pl.when(step == 3)
    def _():
        for o in range(4):
            store(o, w_kv[o // 2, :, (o % 2) * 256 : (o % 2 + 1) * 256])


def project(plan, hidden, by, gain, w_query, w_kv):
    def whole(*shape):
        return pl.BlockSpec(shape, lambda i: (0,) * len(shape))

    small = whole(3, 8, 384)
    return pl.pallas_call(
        project_kernel,
        out_shape=jax.ShapeDtypeStruct((CTX, 32, 256), F32),
        grid=(4,),
        in_specs=[SMEM, small, small, small, small, whole(1, 384)]
        + [
            pl.BlockSpec((384, 1024), lambda i: (0, jnp.minimum(i, 2))),
            whole(2, 384, 512),
        ],
        out_specs=pl.BlockSpec((4, 32, 256), lambda i: (i, 0, 0)),
        scratch_shapes=[pltpu.VMEM((32, 384), F32), pltpu.VMEM((8, 128), F32)],
        cost_estimate=pl.CostEstimate(
            flops=2 * 32 * 384 * 4096, bytes_accessed=384 * 4096 * 2, transcendentals=0
        ),
        compiler_params=params(12),
        name="project",
    )(plan, hidden, *by, gain, w_query, w_kv)


def rotate_kernel(parts, cosine, sine, out):
    total = parts[0]
    for d in range(1, CTX):
        total = total + parts[d]
    row = total[24:32]
    mean = to_rows(row[1:2, :128], 24) / MODEL_WIDTH
    square = to_rows(row[2:3, :128], 24) / MODEL_WIDTH
    scale = lax.rsqrt(square - mean * mean + NORM_EPSILON)
    value = scale * (total[0:24] - mean * row[0:1])
    for h in range(2):
        part = value[:, h * 128 : (h + 1) * 128]
        turned = part * cosine[...] + pltpu.roll(part, 64, 1) * sine[...]
        turned = turned.astype(BF16)
        for d in range(CTX):
            out[d, h] = turned


def rotate(parts, cosine, sine):
    return pl.pallas_call(
        rotate_kernel,
        out_shape=jax.ShapeDtypeStruct((CTX, 2, 24, 128), BF16),
        in_specs=[VMEM] * 3,
        out_specs=VMEM,
        compiler_params=params(8),
        name="rotate",
    )(parts, cosine, sine)


def attend(keys, values, query, position, length):
    rows = 2 * HALF_ROWS
    row = lax.broadcasted_iota(I32, (rows, 128), 0)
    high = row >= HALF_ROWS
    within = jnp.where(high, row - HALF_ROWS, row)
    group = jnp.where(high, 2, 0) + jnp.where(within >= 18, 1, 0)
    q = query.astype(F32)
    wide = jnp.concatenate([jnp.where(group == g, q, 0.0) for g in range(4)], axis=1).astype(BF16)
    score = lax.dot_general(
        wide, keys, (((1,), (1,)), ((), ())), preferred_element_type=F32
    ) * (HEAD_SIZE ** -0.5)
    line = lax.broadcasted_iota(I32, (rows, 1), 0)
    line = jnp.where(line >= HALF_ROWS, line - HALF_ROWS, line)
    visible = position <= length + lax.rem(line, STEPS)
    masked = jnp.where(visible, score, MASKED_SCORE)
    peak = jnp.max(masked, axis=1, keepdims=True)
    weight = jnp.where(visible, jnp.exp(masked - peak), 0.0)
    total = jnp.sum(weight, axis=1, keepdims=True)
    mixed = jnp.dot(weight.astype(BF16), values, preferred_element_type=F32)
    out = jnp.zeros((rows, 128), F32)
    for g in range(4):
        out = out + jnp.where(group == g, mixed[:, g * 128 : (g + 1) * 128], 0.0)
    return [
        message(
            out[h * HALF_ROWS : (h + 1) * HALF_ROWS],
            peak[h * HALF_ROWS : (h + 1) * HALF_ROWS],
            total[h * HALF_ROWS : (h + 1) * HALF_ROWS],
        )
        for h in range(2)
    ]


def message(out, peak, total):
    peak = to_lanes(peak, HALF_ROWS)
    total = to_lanes(total, HALF_ROWS)
    parts = []
    for value, count in ((peak, 3), (total, 2)):
        for _ in range(count):
            part = value.astype(BF16).astype(F32)
            parts.append(part)
            value = value - part
    row = lax.broadcasted_iota(I32, (HALF_ROWS, 128), 0)
    for i, part in enumerate(parts):
        out = jnp.where(row == STAT_ROW + i, part, out)
    return out.astype(BF16)


def blank_message():
    row = lax.broadcasted_iota(I32, (HALF_ROWS, 128), 0)
    return jnp.where(row == STAT_ROW, MASKED_SCORE, 0.0).astype(BF16)


def stay_kernel(plan, cache, query, entries, new_cache, sums):
    s = pl.program_id(0)
    base = lax.axis_index("ctx") * RANGE
    length = plan[NEW_LEN + s]
    stays = plan[STAYS + s] > 0
    some = jnp.logical_and(stays, base < length + STEPS)
    full = jnp.logical_and(some, base + RANGE <= length)

    @pl.when(full)
    def _():
        new_cache[...] = cache[...]

    @pl.when(jnp.logical_and(some, jnp.logical_not(full)))
    def _():
        at = base + lax.broadcasted_iota(I32, (RANGE, 1), 0)
        for kv in range(2):
            block = jnp.where(at < length, cache[kv, 0], jnp.zeros((), BF16))
            for t in range(STEPS):
                block = jnp.where(at == length + t, entries[0, kv, t : t + 1, :], block)
            new_cache[kv, 0] = block

    @pl.when(some)
    def _():
        position = base + lax.broadcasted_iota(I32, (1, RANGE), 1)
        halves = attend(new_cache[0, 0], new_cache[1, 0], query[0], position, length)
        for h in range(2):
            sums[0, h] = halves[h]

    @pl.when(jnp.logical_not(some))
    def _():
        new_cache[...] = jnp.zeros_like(new_cache)
        for h in range(2):
            sums[0, h] = blank_message()


def stay(plan, cache, query, entries):
    return pl.pallas_call(
        stay_kernel,
        out_shape=[
            jax.ShapeDtypeStruct(cache.shape, BF16),
            jax.ShapeDtypeStruct((SLOTS, 2, HALF_ROWS, 128), BF16),
        ],
        grid=(SLOTS,),
        in_specs=[
            SMEM,
            pl.BlockSpec((2, 1, RANGE, FEATURES), lambda s: (0, s, 0, 0)),
            pl.BlockSpec((1, 2 * HALF_ROWS, 128), lambda s: (s, 0, 0)),
            pl.BlockSpec((1, 2, 8, FEATURES), lambda s: (s, 0, 0, 0)),
        ],
        out_specs=[
            pl.BlockSpec((2, 1, RANGE, FEATURES), lambda s: (0, s, 0, 0)),
            pl.BlockSpec((1, 2, HALF_ROWS, 128), lambda s: (s, 0, 0, 0)),
        ],
        cost_estimate=pl.CostEstimate(
            flops=0, bytes_accessed=32 * 1024 * 1024, transcendentals=0
        ),
        compiler_params=params(24),
        name="stay",
    )(plan, cache, query, entries)


def gather_kernel(items, plan, entries, *refs):
    count = 4 * CHUNKS - 2
    arrived, (held, sem) = refs[:count], refs[count:]
    straight = (arrived[:CHUNKS], arrived[CHUNKS : 2 * CHUNKS])
    onward = (arrived[2 * CHUNKS : 3 * CHUNKS - 1], arrived[3 * CHUNKS - 1 :])
    inst = lax.axis_index("inst")

    def fetch(way, chunk, ref, target):
        def one(i, carry):
            code = plan[TARGET + way * LIST + chunk * items + i]
            inside = lax.bitwise_and(code, 63)

            @pl.when(lax.shift_right_arithmetic(code, 6) == target)
            def _():
                place = lax.shift_right_logical(inside, 4)
                c = lax.bitwise_and(inside, 15)
                pltpu.make_async_copy(ref.at[i], held.at[c, place], sem).start()

            return carry

        lax.fori_loop(0, items, one, 0)

    for way, target in ((0, 0), (1, 2)):

        @pl.when(inst == target)
        def _(way=way, target=target):
            for chunk in range(CHUNKS):
                fetch(way, chunk, straight[way][chunk], target)

    @pl.when(inst == 1)
    def _():
        for way in range(2):
            for chunk in range(CHUNKS - 1):
                fetch(way, chunk, onward[way][chunk], 1)

    @pl.when(inst < INST - 1)
    def _():
        for j in range(MOVED):

            def fill(c, carry, j=j):
                pltpu.make_async_copy(arrived[0].at[0], held.at[c, j], sem).start()
                return carry

            lax.fori_loop(plan[COUNT + j], CTX, fill, 0)
        pltpu.make_async_copy(held, held, sem).wait()

    for j in range(MOVED):

        @pl.when(plan[VALID + j] > 0)
        def _(j=j):
            slot = plan[SLOT + j]
            length = plan[LENGTH + j]
            at = lax.broadcasted_iota(I32, (BLOCK, 1), 0)

            def cut(c, carry):
                start = plan[LOGICAL + c] * BLOCK

                @pl.when(start + BLOCK > length)
                def _():
                    for kv in range(2):
                        block = jnp.where(start + at < length, held[c, j, kv], jnp.zeros((), BF16))
                        new = entries[slot, kv]
                        for t in range(STEPS):
                            block = jnp.where(start + at == length + t, new[t : t + 1, :], block)
                        held[c, j, kv] = block

                return carry

            lax.fori_loop(0, CTX, cut, 0)


def gather(items, plan, entries, arrived):
    return pl.pallas_call(
        functools.partial(gather_kernel, items),
        out_shape=jax.ShapeDtypeStruct((CTX, MOVED, 2, BLOCK, FEATURES), BF16),
        in_specs=[SMEM, VMEM] + [HBM] * len(arrived),
        out_specs=VMEM,
        scratch_shapes=[pltpu.SemaphoreType.DMA(())],
        cost_estimate=pl.CostEstimate(flops=0, bytes_accessed=8 * 1024 * 1024, transcendentals=0),
        compiler_params=params(12),
        name="gather",
    )(plan, entries, *arrived)


def moved_kernel(plan, query, held, sums, new_sums):
    new_sums[...] = sums[...]
    lane = lax.broadcasted_iota(I32, (1, RANGE), 1)
    position = jnp.zeros((1, RANGE), I32)
    for c in range(CTX):
        start = plan[LOGICAL + c] * BLOCK
        position = jnp.where(
            lax.shift_right_logical(lane, 5) == c, start + lane - c * BLOCK, position
        )
    for j in range(MOVED):

        @pl.when(plan[VALID + j] > 0)
        def _(j=j):
            slot = plan[SLOT + j]
            keys = held[:, j, 0].reshape(RANGE, FEATURES)
            values = held[:, j, 1].reshape(RANGE, FEATURES)
            halves = attend(keys, values, query[slot], position, plan[LENGTH + j])
            for h in range(2):
                new_sums[slot, h] = halves[h]


def attend_moved(plan, query, held, sums):
    return pl.pallas_call(
        moved_kernel,
        out_shape=jax.ShapeDtypeStruct(sums.shape, BF16),
        in_specs=[SMEM, VMEM, VMEM, VMEM],
        out_specs=VMEM,
        cost_estimate=pl.CostEstimate(flops=0, bytes_accessed=12 * 1024 * 1024, transcendentals=0),
        compiler_params=params(12),
        name="moved",
    )(plan, query, held, sums)


def merge_kernel(parts, out):
    blocks = [parts[d].astype(F32) for d in range(CTX)]
    peaks = []
    totals = []
    for block in blocks:
        stat = block[STAT_ROW : STAT_ROW + 8]
        peaks.append(stat[0:1] + stat[1:2] + stat[2:3])
        totals.append(stat[3:4] + stat[4:5])
    peak = functools.reduce(jnp.maximum, peaks)
    factors = [jnp.exp(p - peak) for p in peaks]
    total = functools.reduce(jnp.add, [f * t for f, t in zip(factors, totals)])
    under = to_rows(jnp.where(total > 0, total, 1.0), HALF_ROWS)
    mixed = functools.reduce(
        jnp.add, [to_rows(f, HALF_ROWS) * b for f, b in zip(factors, blocks)]
    )
    attended = (mixed / under).astype(BF16)
    for d in range(CTX):
        out[d] = attended


def merge(parts):
    return pl.pallas_call(
        merge_kernel,
        out_shape=jax.ShapeDtypeStruct(parts.shape, BF16),
        in_specs=[VMEM],
        out_specs=VMEM,
        compiler_params=params(8),
        name="merge",
    )(parts)


def place_kernel(plan, received, cache, new_cache, held, read_sem, write_sem):
    for j in range(MOVED):

        @pl.when(plan[VALID + j] > 0)
        def _(j=j):
            def one(d, carry):
                rows = pl.ds(pl.multiple_of(plan[WITHIN + d] * BLOCK, BLOCK), BLOCK)
                pltpu.make_async_copy(
                    received.at[d, j], held.at[j, :, rows, :], read_sem.at[j]
                ).start()
                return carry

            lax.fori_loop(0, CTX, one, 0)

    for j in range(MOVED):

        @pl.when(plan[VALID + j] > 0)
        def _(j=j):
            pltpu.make_async_copy(held.at[j], held.at[j], read_sem.at[j]).wait()
            pltpu.make_async_copy(
                held.at[j], new_cache.at[:, plan[SLOT + j]], write_sem.at[j]
            ).start()

    for j in range(MOVED):

        @pl.when(plan[VALID + j] > 0)
        def _(j=j):
            pltpu.make_async_copy(
                held.at[j], new_cache.at[:, plan[SLOT + j]], write_sem.at[j]
            ).wait()


def place(plan, received, cache):
    return pl.pallas_call(
        place_kernel,
        out_shape=jax.ShapeDtypeStruct(cache.shape, BF16),
        in_specs=[SMEM, ANY, HBM],
        out_specs=HBM,
        scratch_shapes=[
            pltpu.VMEM((MOVED, 2, RANGE, FEATURES), BF16),
            pltpu.SemaphoreType.DMA((MOVED,)),
            pltpu.SemaphoreType.DMA((MOVED,)),
        ],
        input_output_aliases={2: 0},
        compiler_params=params(12),
        name="place",
    )(plan, received, cache)


def swap(x):
    return lax.all_to_all(x, "ctx", split_axis=0, concat_axis=0, tiled=True)


def after(*values):
    return lax.optimization_barrier(values)


def shards(
    cache,
    hidden,
    norm_gain,
    w_query,
    key_value_weight,
    w_out,
    lengths,
    dest_inst,
    dest_slot,
    block_order,
):
    by = [lax.ppermute(hidden, "inst", [(INST - 1, i)]) for i in range(INST - 1)]
    plan = make_plan(lengths, dest_inst, dest_slot, block_order)
    *by, plan = after(*by, plan)
    operands = (plan, cache, hidden, by, norm_gain[None], w_query, key_value_weight, w_out)
    return lax.switch(
        plan[NEED], [functools.partial(decode, items) for items in ITEMS], *operands
    )


def angles(plan):
    new_len = plan[NEW_LEN : NEW_LEN + SLOTS]
    token = new_len[None, :] + jnp.arange(STEPS, dtype=I32)[:, None]
    half = HEAD_SIZE // 2
    frequency = ROPE_BASE ** (-jnp.arange(half, dtype=F32) * 2.0 / HEAD_SIZE)
    angle = token.astype(F32).reshape(24, 1) * frequency
    is_value = lax.axis_index("ctx") >= 14
    cosine = jnp.where(is_value, 1.0, jnp.cos(angle))
    sine = jnp.where(is_value, 0.0, jnp.sin(angle))
    return jnp.concatenate([cosine, cosine], axis=1), jnp.concatenate([-sine, sine], axis=1)


def send(items, chunk, plan, cache):
    one, two = pack(chunk, items, plan, cache)
    return (
        lax.ppermute(one, "inst", [(INST - 1, 0)]),
        lax.ppermute(two, "inst", [(INST - 1, 2)]),
        one,
    )


def decode(items, plan, cache, hidden, by, gain, w_query, w_kv, w_out):
    up_0, down_0, packed = send(items, 0, plan, cache)
    hidden, plan, packed = after(hidden, plan, packed)
    cosine, sine = angles(plan)
    projected = project(plan, hidden, by, gain, w_query, w_kv)
    projected, cosine, sine, plan = after(projected, cosine, sine, plan)
    up_1, down_1, packed = send(items, 1, plan, cache)
    parts, up_0, down_0, packed = after(swap(projected), up_0, down_0, packed)
    up_on = lax.ppermute(up_0, "inst", [(0, 1)])
    down_on = lax.ppermute(down_0, "inst", [(2, 1)])
    turned = swap(rotate(parts, cosine, sine))
    turned = turned.reshape(32, STEPS, SLOTS, HEAD_SIZE)
    query = turned[:24].reshape(2, 12, STEPS, SLOTS, HEAD_SIZE).transpose(3, 0, 1, 2, 4)
    query = query.reshape(SLOTS, 2, 36, HEAD_SIZE)
    query = jnp.pad(query, ((0, 0), (0, 0), (0, HALF_ROWS - 36), (0, 0)))
    query = query.reshape(SLOTS, 2 * HALF_ROWS, HEAD_SIZE)
    entries = turned[24:].reshape(2, 4, STEPS, SLOTS, HEAD_SIZE).transpose(3, 0, 2, 1, 4)
    entries = entries.reshape(SLOTS, 2, STEPS, FEATURES)
    entries = jnp.pad(entries, ((0, 0), (0, 0), (0, 8 - STEPS), (0, 0)))

    new_cache, sums = stay(plan, cache, query, entries)
    entries, sums = after(entries, sums)
    held = gather(items, plan, entries, [up_0, up_1, down_0, down_1, up_on, down_on])
    sums = attend_moved(plan, query, held, sums)
    sums, held = after(swap(sums.reshape(CTX, HALF_ROWS, HEAD_SIZE)), held)
    sums, received = after(sums, swap(held))
    attended = swap(merge(sums))
    new_cache = place(plan, received, new_cache)
    attended, new_cache = after(attended, new_cache)

    attended = attended[:, :36].reshape(SLOTS, 2, 12, STEPS, HEAD_SIZE)
    attended = attended.transpose(3, 0, 1, 2, 4).reshape(24, 24 * HEAD_SIZE)
    projected = jnp.dot(attended, w_out, preferred_element_type=F32)
    mine, other = projected[:, :192], projected[:, 192:]
    first = lax.axis_index("head") == 0
    keep = jnp.where(first, mine, other)
    send_half = jnp.where(first, other, mine).astype(BF16)
    got = lax.ppermute(send_half, "head", [(0, 1), (1, 0)])
    attn_out = (keep + got.astype(F32)).astype(BF16)
    return new_cache, attn_out.reshape(STEPS, SLOTS, 192)


def solution(mesh):
    placed = (
        P(None, "inst", "ctx", "head"),
        P(None, "inst", "ctx"),
        P("ctx"),
        P("ctx", "head"),
        P(None, "ctx", "head"),
        P("head", "ctx"),
        P(),
        P(),
        P(),
        P(),
    )
    return jax.shard_map(
        shards,
        mesh=mesh,
        in_specs=placed,
        out_specs=(P(None, "inst", "ctx", "head"), P(None, "inst", ("ctx", "head"))),
        check_vma=False,
    )
```

```python
import functools

import jax
import jax.numpy as jnp
from jax import lax
from jax.experimental import pallas as pl
from jax.experimental.pallas import tpu as pltpu
from jax.sharding import PartitionSpec as P

MODEL_WIDTH = 6144
HEAD_SIZE = 128
ROPE_BASE = 500000.0
NORM_EPSILON = 1e-05
MASKED_SCORE = -1e30

INST = 4
CTX = 16
SLOTS = 8
STEPS = 3
MOVED = 3
BLOCK = 32
RANGE = 512
FEATURES = 512
HALF_ROWS = 48
STAT_ROW = 40
CHUNKS = 2
ITEMS = ((16, 24), (20, 24), (23, 25), (26, 28), (32, 40))
BF16 = jnp.bfloat16
F32 = jnp.float32
I32 = jnp.int32

NEW_LEN, STAYS, REQUEST = 0, 8, 16
VALID, SLOT, LENGTH, COUNT = 24, 28, 32, 36
STORED, LOGICAL = 48, 64
NEED = 80
SOURCE, TARGET = 128, 272
PLAN_SIZE = 416
LIST = 72

VMEM = pl.BlockSpec(memory_space=pltpu.VMEM)
SMEM = pl.BlockSpec(memory_space=pltpu.SMEM)
ANY = pl.BlockSpec(memory_space=pl.ANY)
HBM = pl.BlockSpec(memory_space=pltpu.HBM)


def params(mib):
    return pltpu.CompilerParams(vmem_limit_bytes=mib * 1024 * 1024)


def plan_kernel(lengths, dest_inst, dest_slot, order, plan):
    inst = lax.axis_index("inst")
    ctx = lax.axis_index("ctx")

    for s in range(SLOTS):
        own = jnp.where(inst == INST - 1, 0, lengths[inst * SLOTS + s])
        plan[NEW_LEN + s] = own
        plan[STAYS + s] = jnp.where(own > 0, 1, 0)
        plan[REQUEST + s] = -1
    for j in range(4):
        plan[VALID + j] = 0
        plan[SLOT + j] = 0
        plan[LENGTH + j] = 0
        plan[COUNT + j] = 0
    for b in range(CTX):
        q = order[ctx * CTX + b]
        plan[STORED + lax.shift_right_logical(q, 4)] = b
        plan[LOGICAL + lax.shift_right_logical(q, 4)] = q

    counts = []
    total = [jnp.int32(0)] * 3
    for r in range(SLOTS):
        long = lengths[(INST - 1) * SLOTS + r]
        count = lax.shift_right_logical(long + STEPS + RANGE - 1, 9)
        counts.append(count)
        to = dest_inst[r]
        total = [total[i] + jnp.where(to == i, count, 0) for i in range(3)]
    def weigh(part, best):
        rest = total[1] - part
        need = jnp.maximum(part + total[0], rest + total[2])
        onward = jnp.maximum(part, rest)
        size = jnp.int32(0)
        for one, two in ITEMS[:-1]:
            small = jnp.logical_or(need > one + two, onward > one)
            size = size + jnp.where(small, 1, 0)
        size = size * 256 + need + jnp.where(onward > ITEMS[-1][0], 128, 0)
        better = size < best[0]
        return jnp.where(better, size, best[0]), jnp.where(better, part, best[1])

    size, split = lax.fori_loop(0, total[1] + 1, weigh, (jnp.int32(4096), jnp.int32(0)))
    size = lax.shift_right_logical(size, 8)
    rest = total[1] - split
    plan[NEED] = size

    done = [jnp.int32(0)] * 3
    rank = [jnp.int32(0)] * 3
    for r in range(SLOTS):
        to = dest_inst[r]
        count = counts[r]
        base = jnp.where(to == 0, done[0], jnp.where(to == 1, done[1], done[2]))
        place = jnp.where(to == 0, rank[0], jnp.where(to == 1, rank[1], rank[2]))

        front = jnp.where(to == 0, split, jnp.where(to == 1, 0, LIST + rest)) + base
        back = jnp.where(to == 1, LIST + base - split, front)
        turn = split - base
        source = r * CTX
        target = to * 64 + place * CTX

        def put(c, carry, front=front, back=back, turn=turn, source=source, target=target):
            p = c + jnp.where(c < turn, front, back)
            plan[SOURCE + p] = source + c
            plan[TARGET + p] = target + c
            return carry

        lax.fori_loop(0, count, put, 0)

        @pl.when(to == inst)
        def _(r=r, place=place, count=count):
            long = lengths[(INST - 1) * SLOTS + r]
            slot = dest_slot[r]
            plan[NEW_LEN + slot] = long
            plan[STAYS + slot] = 0
            plan[REQUEST + slot] = r
            plan[VALID + place] = jnp.where(long > 0, 1, 0)
            plan[SLOT + place] = slot
            plan[LENGTH + place] = long
            plan[COUNT + place] = count

        done = [done[i] + jnp.where(to == i, count, 0) for i in range(3)]
        rank = [rank[i] + jnp.where(to == i, 1, 0) for i in range(3)]

    def clear(p, carry):
        plan[SOURCE + p] = 0
        plan[TARGET + p] = -1
        return carry

    lax.fori_loop(split + total[0], LIST, clear, 0)
    lax.fori_loop(LIST + rest + total[2], 2 * LIST, clear, 0)


def make_plan(lengths, dest_inst, dest_slot, order):
    return pl.pallas_call(
        plan_kernel,
        out_shape=jax.ShapeDtypeStruct((PLAN_SIZE,), I32),
        in_specs=[SMEM] * 4,
        out_specs=SMEM,
        name="plan",
    )(lengths, dest_inst, dest_slot, order)


def pack_kernel(first, items, plan, cache, up, down, held, read_sem, write_sem):
    @pl.when(lax.axis_index("inst") == INST - 1)
    def _():
        for way in range(2):

            def read(i, carry, way=way):
                code = plan[SOURCE + way * LIST + first + i]
                r = lax.shift_right_logical(code, 4)
                stored = plan[STORED + lax.bitwise_and(code, 15)]
                rows = pl.ds(pl.multiple_of(stored * BLOCK, BLOCK), BLOCK)
                pltpu.make_async_copy(
                    cache.at[:, r, rows, :], held.at[way, i], read_sem.at[way]
                ).start()
                return carry

            lax.fori_loop(0, items, read, 0)
        for way, out in enumerate((up, down)):
            pltpu.make_async_copy(held.at[way], held.at[way], read_sem.at[way]).wait()
            pltpu.make_async_copy(held.at[way], out, write_sem.at[way]).start()
        for way, out in enumerate((up, down)):
            pltpu.make_async_copy(held.at[way], out, write_sem.at[way]).wait()


def pack(first, items, plan, cache):
    shape = (items, 2, BLOCK, FEATURES)
    return pl.pallas_call(
        functools.partial(pack_kernel, first, items),
        out_shape=[jax.ShapeDtypeStruct(shape, BF16)] * 2,
        in_specs=[SMEM, HBM],
        out_specs=[HBM, HBM],
        scratch_shapes=[
            pltpu.VMEM((2, *shape), BF16),
            pltpu.SemaphoreType.DMA((2,)),
            pltpu.SemaphoreType.DMA((2,)),
        ],
        cost_estimate=pl.CostEstimate(
            flops=0, bytes_accessed=8 * items * BLOCK * FEATURES * 2, transcendentals=0
        ),
        compiler_params=params(56),
        name="pack",
    )(plan, cache)


def to_lanes(column, rows):
    shape = (rows, 128)
    same = lax.broadcasted_iota(I32, shape, 0) == lax.broadcasted_iota(I32, shape, 1)
    return jnp.sum(jnp.where(same, column, 0.0), axis=0, keepdims=True)


def to_rows(lanes, rows):
    shape = (rows, 128)
    same = lax.broadcasted_iota(I32, shape, 0) == lax.broadcasted_iota(I32, shape, 1)
    return jnp.sum(jnp.where(same, lanes, 0.0), axis=1, keepdims=True)


def project_kernel(
    plan, order, hidden, by0, by1, by2, gain, w_query, w_kv, out, within, lhs, stats
):
    step = pl.program_id(0)

    @pl.when(step == 0)
    def _():
        row = lax.broadcasted_iota(I32, (SLOTS, 1), 0)
        request = jnp.full((SLOTS, 1), -1, I32)
        for s in range(SLOTS):
            request = jnp.where(row == s, plan[REQUEST + s], request)
        scale = gain[...].astype(F32)
        sums = []
        squares = []
        for t in range(STEPS):
            x = hidden[t].astype(F32)
            moved = by0[t].astype(F32) + by1[t].astype(F32) + by2[t].astype(F32)
            for r in range(SLOTS):
                x = jnp.where(request == r, moved[r : r + 1, :], x)
            sums.append(jnp.sum(x, axis=1, keepdims=True))
            squares.append(jnp.sum(x * x, axis=1, keepdims=True))
            lhs[t * SLOTS : (t + 1) * SLOTS, :] = x * scale
        lhs[24:32, :] = jnp.where(row == 0, scale, 0.0)
        sum_lanes = to_lanes(jnp.concatenate(sums, axis=0), 24)
        square_lanes = to_lanes(jnp.concatenate(squares, axis=0), 24)
        stats[...] = jnp.where(row == 1, sum_lanes, jnp.where(row == 2, square_lanes, 0.0))
        ctx = lax.axis_index("ctx")

        def search(d, carry):
            found = jnp.int32(0)
            for b in range(CTX):
                q = order[d * CTX + b]
                mine = lax.shift_right_logical(q, 4) == ctx
                found = jnp.where(mine, lax.bitwise_and(q, CTX - 1), found)
            within[d] = found
            return carry

        lax.fori_loop(0, CTX, search, 0)

    left = lhs[...].astype(BF16)
    tail = stats[...]
    row = lax.broadcasted_iota(I32, (SLOTS, 256), 0)
    wide = jnp.concatenate([tail, tail], axis=1)

    def store(o, weight):
        got = jnp.dot(left, weight, preferred_element_type=F32)
        out[o, 0:24, :] = got[0:24]
        out[o, 24:32, :] = jnp.where(row == 0, got[24:32], wide)

    @pl.when(step < 3)
    def _():
        for o in range(4):
            store(o, w_query[:, o * 256 : (o + 1) * 256])

    @pl.when(step == 3)
    def _():
        for o in range(4):
            store(o, w_kv[o // 2, :, (o % 2) * 256 : (o % 2 + 1) * 256])


def project(plan, order, hidden, by, gain, w_query, w_kv):
    def whole(*shape):
        return pl.BlockSpec(shape, lambda i: (0,) * len(shape))

    small = whole(3, 8, 384)
    return pl.pallas_call(
        project_kernel,
        out_shape=[
            jax.ShapeDtypeStruct((CTX, 32, 256), F32),
            jax.ShapeDtypeStruct((CTX,), I32),
        ],
        grid=(4,),
        in_specs=[SMEM, SMEM, small, small, small, small, whole(1, 384)]
        + [
            pl.BlockSpec((384, 1024), lambda i: (0, jnp.minimum(i, 2))),
            whole(2, 384, 512),
        ],
        out_specs=[pl.BlockSpec((4, 32, 256), lambda i: (i, 0, 0)), SMEM],
        scratch_shapes=[pltpu.VMEM((32, 384), F32), pltpu.VMEM((8, 128), F32)],
        cost_estimate=pl.CostEstimate(
            flops=2 * 32 * 384 * 4096, bytes_accessed=384 * 4096 * 2, transcendentals=0
        ),
        compiler_params=params(12),
        name="project",
    )(plan, order, hidden, *by, gain, w_query, w_kv)


def rotate_kernel(parts, cosine, sine, out):
    total = parts[0]
    for d in range(1, CTX):
        total = total + parts[d]
    row = total[24:32]
    mean = to_rows(row[1:2, :128], 24) / MODEL_WIDTH
    square = to_rows(row[2:3, :128], 24) / MODEL_WIDTH
    scale = lax.rsqrt(square - mean * mean + NORM_EPSILON)
    value = scale * (total[0:24] - mean * row[0:1])
    for h in range(2):
        part = value[:, h * 128 : (h + 1) * 128]
        turned = part * cosine[...] + pltpu.roll(part, 64, 1) * sine[...]
        turned = turned.astype(BF16)
        for d in range(CTX):
            out[d, h] = turned


def rotate(parts, cosine, sine):
    return pl.pallas_call(
        rotate_kernel,
        out_shape=jax.ShapeDtypeStruct((CTX, 2, 24, 128), BF16),
        in_specs=[VMEM] * 3,
        out_specs=VMEM,
        compiler_params=params(8),
        name="rotate",
    )(parts, cosine, sine)


def attend(keys, values, query, position, length):
    rows = 2 * HALF_ROWS
    row = lax.broadcasted_iota(I32, (rows, 128), 0)
    high = row >= HALF_ROWS
    within = jnp.where(high, row - HALF_ROWS, row)
    group = jnp.where(high, 2, 0) + jnp.where(within >= 18, 1, 0)
    q = query.astype(F32)
    wide = jnp.concatenate([jnp.where(group == g, q, 0.0) for g in range(4)], axis=1).astype(BF16)
    score = lax.dot_general(
        wide, keys, (((1,), (1,)), ((), ())), preferred_element_type=F32
    ) * (HEAD_SIZE ** -0.5)
    line = lax.broadcasted_iota(I32, (rows, 1), 0)
    line = jnp.where(line >= HALF_ROWS, line - HALF_ROWS, line)
    visible = position <= length + lax.rem(line, STEPS)
    masked = jnp.where(visible, score, MASKED_SCORE)
    peak = jnp.max(masked, axis=1, keepdims=True)
    weight = jnp.where(visible, jnp.exp(masked - peak), 0.0)
    total = jnp.sum(weight, axis=1, keepdims=True)
    mixed = jnp.dot(weight.astype(BF16), values, preferred_element_type=F32)
    out = jnp.zeros((rows, 128), F32)
    for g in range(4):
        out = out + jnp.where(group == g, mixed[:, g * 128 : (g + 1) * 128], 0.0)
    return [
        message(
            out[h * HALF_ROWS : (h + 1) * HALF_ROWS],
            peak[h * HALF_ROWS : (h + 1) * HALF_ROWS],
            total[h * HALF_ROWS : (h + 1) * HALF_ROWS],
        )
        for h in range(2)
    ]


def message(out, peak, total):
    peak = to_lanes(peak, HALF_ROWS)
    total = to_lanes(total, HALF_ROWS)
    parts = []
    for value, count in ((peak, 3), (total, 2)):
        for _ in range(count):
            part = value.astype(BF16).astype(F32)
            parts.append(part)
            value = value - part
    row = lax.broadcasted_iota(I32, (HALF_ROWS, 128), 0)
    for i, part in enumerate(parts):
        out = jnp.where(row == STAT_ROW + i, part, out)
    return out.astype(BF16)


def blank_message():
    row = lax.broadcasted_iota(I32, (HALF_ROWS, 128), 0)
    return jnp.where(row == STAT_ROW, MASKED_SCORE, 0.0).astype(BF16)


def stay_kernel(plan, cache, query, entries, new_cache, sums):
    s = pl.program_id(0)
    base = lax.axis_index("ctx") * RANGE
    length = plan[NEW_LEN + s]
    stays = plan[STAYS + s] > 0
    some = jnp.logical_and(stays, base < length + STEPS)
    full = jnp.logical_and(some, base + RANGE <= length)

    @pl.when(full)
    def _():
        new_cache[...] = cache[...]

    @pl.when(jnp.logical_and(some, jnp.logical_not(full)))
    def _():
        at = base + lax.broadcasted_iota(I32, (RANGE, 1), 0)
        for kv in range(2):
            block = jnp.where(at < length, cache[kv, 0], jnp.zeros((), BF16))
            for t in range(STEPS):
                block = jnp.where(at == length + t, entries[0, kv, t : t + 1, :], block)
            new_cache[kv, 0] = block

    @pl.when(some)
    def _():
        position = base + lax.broadcasted_iota(I32, (1, RANGE), 1)
        halves = attend(new_cache[0, 0], new_cache[1, 0], query[0], position, length)
        for h in range(2):
            sums[0, h] = halves[h]

    @pl.when(jnp.logical_not(some))
    def _():
        new_cache[...] = jnp.zeros_like(new_cache)
        for h in range(2):
            sums[0, h] = blank_message()


def stay(plan, cache, query, entries):
    return pl.pallas_call(
        stay_kernel,
        out_shape=[
            jax.ShapeDtypeStruct(cache.shape, BF16),
            jax.ShapeDtypeStruct((SLOTS, 2, HALF_ROWS, 128), BF16),
        ],
        grid=(SLOTS,),
        in_specs=[
            SMEM,
            pl.BlockSpec((2, 1, RANGE, FEATURES), lambda s: (0, s, 0, 0)),
            pl.BlockSpec((1, 2 * HALF_ROWS, 128), lambda s: (s, 0, 0)),
            pl.BlockSpec((1, 2, 8, FEATURES), lambda s: (s, 0, 0, 0)),
        ],
        out_specs=[
            pl.BlockSpec((2, 1, RANGE, FEATURES), lambda s: (0, s, 0, 0)),
            pl.BlockSpec((1, 2, HALF_ROWS, 128), lambda s: (s, 0, 0, 0)),
        ],
        cost_estimate=pl.CostEstimate(
            flops=0, bytes_accessed=32 * 1024 * 1024, transcendentals=0
        ),
        compiler_params=params(24),
        name="stay",
    )(plan, cache, query, entries)


def gather_kernel(items, plan, entries, *refs):
    count = 4 * CHUNKS - 2
    arrived, (held, sem) = refs[:count], refs[count:]
    straight = (arrived[:CHUNKS], arrived[CHUNKS : 2 * CHUNKS])
    onward = (arrived[2 * CHUNKS : 3 * CHUNKS - 1], arrived[3 * CHUNKS - 1 :])
    inst = lax.axis_index("inst")

    def fetch(way, chunk, ref, target):
        first = sum(items[:chunk])

        def one(i, carry):
            code = plan[TARGET + way * LIST + first + i]
            inside = lax.bitwise_and(code, 63)

            @pl.when(lax.shift_right_arithmetic(code, 6) == target)
            def _():
                place = lax.shift_right_logical(inside, 4)
                c = lax.bitwise_and(inside, 15)
                pltpu.make_async_copy(ref.at[i], held.at[c, place], sem.at[c, place]).start()

            return carry

        lax.fori_loop(0, items[chunk], one, 0)

    for way, target in ((0, 0), (1, 2)):

        @pl.when(inst == target)
        def _(way=way, target=target):
            for chunk in range(CHUNKS):
                fetch(way, chunk, straight[way][chunk], target)

    @pl.when(inst == 1)
    def _():
        for way in range(2):
            for chunk in range(CHUNKS - 1):
                fetch(way, chunk, onward[way][chunk], 1)

    for j in range(MOVED):

        @pl.when(plan[VALID + j] > 0)
        def _(j=j):
            slot = plan[SLOT + j]
            length = plan[LENGTH + j]
            count = plan[COUNT + j]
            at = lax.broadcasted_iota(I32, (BLOCK, 1), 0)

            def cut(c, carry):
                start = plan[LOGICAL + c] * BLOCK

                @pl.when(c < count)
                def _():
                    pltpu.make_async_copy(held.at[c, j], held.at[c, j], sem.at[c, j]).wait()

                @pl.when(start >= length + STEPS)
                def _():
                    held[c, j] = jnp.zeros((2, BLOCK, FEATURES), BF16)

                @pl.when(jnp.logical_and(start + BLOCK > length, start < length + STEPS))
                def _():
                    for kv in range(2):
                        block = jnp.where(start + at < length, held[c, j, kv], jnp.zeros((), BF16))
                        new = entries[slot, kv]
                        for t in range(STEPS):
                            block = jnp.where(start + at == length + t, new[t : t + 1, :], block)
                        held[c, j, kv] = block

                return carry

            lax.fori_loop(0, CTX, cut, 0)


def gather(items, plan, entries, arrived):
    return pl.pallas_call(
        functools.partial(gather_kernel, items),
        out_shape=jax.ShapeDtypeStruct((CTX, MOVED, 2, BLOCK, FEATURES), BF16),
        in_specs=[SMEM, VMEM] + [ANY] * len(arrived),
        out_specs=VMEM,
        scratch_shapes=[pltpu.SemaphoreType.DMA((CTX, MOVED))],
        cost_estimate=pl.CostEstimate(flops=0, bytes_accessed=8 * 1024 * 1024, transcendentals=0),
        compiler_params=params(12),
        name="gather",
    )(plan, entries, *arrived)


def moved_kernel(plan, query, held, sums, new_sums):
    new_sums[...] = sums[...]
    lane = lax.broadcasted_iota(I32, (1, RANGE), 1)
    position = jnp.zeros((1, RANGE), I32)
    for c in range(CTX):
        start = plan[LOGICAL + c] * BLOCK
        position = jnp.where(
            lax.shift_right_logical(lane, 5) == c, start + lane - c * BLOCK, position
        )
    for j in range(MOVED):

        @pl.when(plan[VALID + j] > 0)
        def _(j=j):
            slot = plan[SLOT + j]
            keys = held[:, j, 0].reshape(RANGE, FEATURES)
            values = held[:, j, 1].reshape(RANGE, FEATURES)
            halves = attend(keys, values, query[slot], position, plan[LENGTH + j])
            for h in range(2):
                new_sums[slot, h] = halves[h]


def attend_moved(plan, query, held, sums):
    return pl.pallas_call(
        moved_kernel,
        out_shape=jax.ShapeDtypeStruct(sums.shape, BF16),
        in_specs=[SMEM, VMEM, VMEM, VMEM],
        out_specs=VMEM,
        cost_estimate=pl.CostEstimate(flops=0, bytes_accessed=12 * 1024 * 1024, transcendentals=0),
        compiler_params=params(12),
        name="moved",
    )(plan, query, held, sums)


def merge_kernel(parts, out):
    blocks = [parts[d].astype(F32) for d in range(CTX)]
    peaks = []
    totals = []
    for block in blocks:
        stat = block[STAT_ROW : STAT_ROW + 8]
        peaks.append(stat[0:1] + stat[1:2] + stat[2:3])
        totals.append(stat[3:4] + stat[4:5])
    peak = functools.reduce(jnp.maximum, peaks)
    factors = [jnp.exp(p - peak) for p in peaks]
    total = functools.reduce(jnp.add, [f * t for f, t in zip(factors, totals)])
    under = to_rows(jnp.where(total > 0, total, 1.0), HALF_ROWS)
    mixed = functools.reduce(
        jnp.add, [to_rows(f, HALF_ROWS) * b for f, b in zip(factors, blocks)]
    )
    attended = (mixed / under).astype(BF16)
    for d in range(CTX):
        out[d] = attended


def merge(parts):
    return pl.pallas_call(
        merge_kernel,
        out_shape=jax.ShapeDtypeStruct(parts.shape, BF16),
        in_specs=[VMEM],
        out_specs=VMEM,
        compiler_params=params(8),
        name="merge",
    )(parts)


def place_kernel(plan, within, received, cache, new_cache, held, read_sem, write_sem):
    for j in range(MOVED):

        @pl.when(plan[VALID + j] > 0)
        def _(j=j):
            def one(d, carry):
                rows = pl.ds(pl.multiple_of(within[d] * BLOCK, BLOCK), BLOCK)
                pltpu.make_async_copy(
                    received.at[d, j], held.at[j, :, rows, :], read_sem.at[j]
                ).start()
                return carry

            lax.fori_loop(0, CTX, one, 0)

    for j in range(MOVED):

        @pl.when(plan[VALID + j] > 0)
        def _(j=j):
            pltpu.make_async_copy(held.at[j], held.at[j], read_sem.at[j]).wait()
            pltpu.make_async_copy(
                held.at[j], new_cache.at[:, plan[SLOT + j]], write_sem.at[j]
            ).start()

    for j in range(MOVED):

        @pl.when(plan[VALID + j] > 0)
        def _(j=j):
            pltpu.make_async_copy(
                held.at[j], new_cache.at[:, plan[SLOT + j]], write_sem.at[j]
            ).wait()


def place(plan, within, received, cache):
    return pl.pallas_call(
        place_kernel,
        out_shape=jax.ShapeDtypeStruct(cache.shape, BF16),
        in_specs=[SMEM, SMEM, ANY, HBM],
        out_specs=HBM,
        scratch_shapes=[
            pltpu.VMEM((MOVED, 2, RANGE, FEATURES), BF16),
            pltpu.SemaphoreType.DMA((MOVED,)),
            pltpu.SemaphoreType.DMA((MOVED,)),
        ],
        input_output_aliases={3: 0},
        compiler_params=params(12),
        name="place",
    )(plan, within, received, cache)


def swap(x):
    return lax.all_to_all(x, "ctx", split_axis=0, concat_axis=0, tiled=True)


def after(*values):
    return lax.optimization_barrier(values)


def shards(
    cache,
    hidden,
    norm_gain,
    w_query,
    key_value_weight,
    w_out,
    lengths,
    dest_inst,
    dest_slot,
    block_order,
):
    by = [up(hidden), down(hidden)]
    by.append(lax.ppermute(by[0], "inst", [(0, 1)]))
    plan = make_plan(lengths, dest_inst, dest_slot, block_order)
    *by, plan = after(*by, plan)
    operands = (
        plan, block_order, cache, hidden, by, norm_gain[None], w_query, key_value_weight, w_out
    )
    return lax.switch(
        plan[NEED], [functools.partial(decode, items) for items in ITEMS], *operands
    )


def angles(plan):
    new_len = plan[NEW_LEN : NEW_LEN + SLOTS]
    token = new_len[None, :] + jnp.arange(STEPS, dtype=I32)[:, None]
    half = HEAD_SIZE // 2
    frequency = ROPE_BASE ** (-jnp.arange(half, dtype=F32) * 2.0 / HEAD_SIZE)
    angle = token.astype(F32).reshape(24, 1) * frequency
    is_value = lax.axis_index("ctx") >= 14
    cosine = jnp.where(is_value, 1.0, jnp.cos(angle))
    sine = jnp.where(is_value, 0.0, jnp.sin(angle))
    return jnp.concatenate([cosine, cosine], axis=1), jnp.concatenate([-sine, sine], axis=1)


def up(x):
    return lax.ppermute(x, "inst", [(INST - 1, 0)])


def down(x):
    return lax.ppermute(x, "inst", [(INST - 1, 2)])


def pass_on(from_up, from_down):
    return lax.ppermute(from_up, "inst", [(0, 1)]), lax.ppermute(from_down, "inst", [(2, 1)])


def decode(items, plan, order, cache, hidden, by, gain, w_query, w_kv, w_out):
    packed_up, packed_down = pack(0, items[0], plan, cache)
    up_0, down_0 = up(packed_up), down(packed_down)
    hidden, plan, packed_up = after(hidden, plan, packed_up)
    cosine, sine = angles(plan)
    projected, within = project(plan, order, hidden, by, gain, w_query, w_kv)
    projected, cosine, sine, plan = after(projected, cosine, sine, plan)
    packed_up, packed_down = pack(items[0], items[1], plan, cache)
    parts, up_0, down_0, packed_up, packed_down = after(
        swap(projected), up_0, down_0, packed_up, packed_down
    )
    up_1, down_1 = up(packed_up), down(packed_down)
    up_on, down_on = pass_on(up_0, down_0)
    turned = swap(rotate(parts, cosine, sine))
    turned = turned.reshape(32, STEPS, SLOTS, HEAD_SIZE)
    query = turned[:24].reshape(2, 12, STEPS, SLOTS, HEAD_SIZE).transpose(3, 0, 1, 2, 4)
    query = query.reshape(SLOTS, 2, 36, HEAD_SIZE)
    query = jnp.pad(query, ((0, 0), (0, 0), (0, HALF_ROWS - 36), (0, 0)))
    query = query.reshape(SLOTS, 2 * HALF_ROWS, HEAD_SIZE)
    entries = turned[24:].reshape(2, 4, STEPS, SLOTS, HEAD_SIZE).transpose(3, 0, 2, 1, 4)
    entries = entries.reshape(SLOTS, 2, STEPS, FEATURES)
    entries = jnp.pad(entries, ((0, 0), (0, 0), (0, 8 - STEPS), (0, 0)))

    new_cache, sums = stay(plan, cache, query, entries)
    entries, sums = after(entries, sums)
    arrived = [up_0, up_1, down_0, down_1, up_on, down_on]
    held = gather(items, plan, entries, arrived)
    sums = attend_moved(plan, query, held, sums)
    sums, held = after(swap(sums.reshape(CTX, HALF_ROWS, HEAD_SIZE)), held)
    sums, received = after(sums, swap(held))
    attended = swap(merge(sums))
    new_cache = place(plan, within, received, new_cache)
    attended, new_cache = after(attended, new_cache)

    attended = attended[:, :36].reshape(SLOTS, 2, 12, STEPS, HEAD_SIZE)
    attended = attended.transpose(3, 0, 1, 2, 4).reshape(24, 24 * HEAD_SIZE)
    projected = jnp.dot(attended, w_out, preferred_element_type=F32)
    mine, other = projected[:, :192], projected[:, 192:]
    first = lax.axis_index("head") == 0
    keep = jnp.where(first, mine, other)
    send_half = jnp.where(first, other, mine).astype(BF16)
    got = lax.ppermute(send_half, "head", [(0, 1), (1, 0)])
    attn_out = (keep + got.astype(F32)).astype(BF16)
    return new_cache, attn_out.reshape(STEPS, SLOTS, 192)


def solution(mesh):
    placed = (
        P(None, "inst", "ctx", "head"),
        P(None, "inst", "ctx"),
        P("ctx"),
        P("ctx", "head"),
        P(None, "ctx", "head"),
        P("head", "ctx"),
        P(),
        P(),
        P(),
        P(),
    )
    return jax.shard_map(
        shards,
        mesh=mesh,
        in_specs=placed,
        out_specs=(P(None, "inst", "ctx", "head"), P(None, "inst", ("ctx", "head"))),
        check_vma=False,
    )
```

```python
import functools

import jax
import jax.numpy as jnp
from jax import lax
from jax.experimental import pallas as pl
from jax.experimental.pallas import tpu as pltpu
from jax.sharding import PartitionSpec as P

MODEL_WIDTH = 6144
HEAD_SIZE = 128
ROPE_BASE = 500000.0
NORM_EPSILON = 1e-05
MASKED_SCORE = -1e30

INST = 4
CTX = 16
SLOTS = 8
STEPS = 3
MOVED = 3
BLOCK = 32
RANGE = 512
FEATURES = 512
HALF_ROWS = 48
STAT_ROW = 40
CHUNKS = 2
ITEMS = ((22, 26), (27, 31), (32, 40))
BF16 = jnp.bfloat16
F32 = jnp.float32
I32 = jnp.int32

NEW_LEN, STAYS, REQUEST = 0, 8, 16
VALID, SLOT, LENGTH, COUNT = 24, 28, 32, 36
STORED, LOGICAL = 48, 64
NEED = 80
SOURCE, TARGET = 128, 272
PLAN_SIZE = 416
LIST = 72

VMEM = pl.BlockSpec(memory_space=pltpu.VMEM)
SMEM = pl.BlockSpec(memory_space=pltpu.SMEM)
ANY = pl.BlockSpec(memory_space=pl.ANY)
HBM = pl.BlockSpec(memory_space=pltpu.HBM)


def params(mib):
    return pltpu.CompilerParams(vmem_limit_bytes=mib * 1024 * 1024)


def plan_kernel(lengths, dest_inst, dest_slot, order, plan):
    inst = lax.axis_index("inst")
    ctx = lax.axis_index("ctx")

    for s in range(SLOTS):
        own = jnp.where(inst == INST - 1, 0, lengths[inst * SLOTS + s])
        plan[NEW_LEN + s] = own
        plan[STAYS + s] = jnp.where(own > 0, 1, 0)
        plan[REQUEST + s] = -1
    for j in range(4):
        plan[VALID + j] = 0
        plan[SLOT + j] = 0
        plan[LENGTH + j] = 0
        plan[COUNT + j] = 0
    for b in range(CTX):
        q = order[ctx * CTX + b]
        plan[STORED + lax.shift_right_logical(q, 4)] = b
        plan[LOGICAL + lax.shift_right_logical(q, 4)] = q

    counts = []
    total = [jnp.int32(0)] * 3
    for r in range(SLOTS):
        long = lengths[(INST - 1) * SLOTS + r]
        count = lax.shift_right_logical(long + STEPS + RANGE - 1, 9)
        counts.append(count)
        to = dest_inst[r]
        total = [total[i] + jnp.where(to == i, count, 0) for i in range(3)]
    def weigh(part, best):
        rest = total[1] - part
        need = jnp.maximum(part + total[0], rest + total[2])
        onward = jnp.maximum(part, rest)
        size = jnp.int32(0)
        for one, two in ITEMS[:-1]:
            small = jnp.logical_or(need > one + two, onward > one)
            size = size + jnp.where(small, 1, 0)
        size = size * 256 + need + jnp.where(onward > ITEMS[-1][0], 128, 0)
        better = size < best[0]
        return jnp.where(better, size, best[0]), jnp.where(better, part, best[1])

    size, split = lax.fori_loop(0, total[1] + 1, weigh, (jnp.int32(4096), jnp.int32(0)))
    size = lax.shift_right_logical(size, 8)
    rest = total[1] - split
    plan[NEED] = size

    done = [jnp.int32(0)] * 3
    rank = [jnp.int32(0)] * 3
    for r in range(SLOTS):
        to = dest_inst[r]
        count = counts[r]
        base = jnp.where(to == 0, done[0], jnp.where(to == 1, done[1], done[2]))
        place = jnp.where(to == 0, rank[0], jnp.where(to == 1, rank[1], rank[2]))

        front = jnp.where(to == 0, split, jnp.where(to == 1, 0, LIST + rest)) + base
        back = jnp.where(to == 1, LIST + base - split, front)
        turn = split - base
        source = r * CTX
        target = to * 64 + place * CTX

        def put(c, carry, front=front, back=back, turn=turn, source=source, target=target):
            p = c + jnp.where(c < turn, front, back)
            plan[SOURCE + p] = source + c
            plan[TARGET + p] = target + c
            return carry

        lax.fori_loop(0, count, put, 0)

        @pl.when(to == inst)
        def _(r=r, place=place, count=count):
            long = lengths[(INST - 1) * SLOTS + r]
            slot = dest_slot[r]
            plan[NEW_LEN + slot] = long
            plan[STAYS + slot] = 0
            plan[REQUEST + slot] = r
            plan[VALID + place] = jnp.where(long > 0, 1, 0)
            plan[SLOT + place] = slot
            plan[LENGTH + place] = long
            plan[COUNT + place] = count

        done = [done[i] + jnp.where(to == i, count, 0) for i in range(3)]
        rank = [rank[i] + jnp.where(to == i, 1, 0) for i in range(3)]

    def clear(p, carry):
        plan[SOURCE + p] = 0
        plan[TARGET + p] = -1
        return carry

    lax.fori_loop(split + total[0], LIST, clear, 0)
    lax.fori_loop(LIST + rest + total[2], 2 * LIST, clear, 0)


def make_plan(lengths, dest_inst, dest_slot, order):
    return pl.pallas_call(
        plan_kernel,
        out_shape=jax.ShapeDtypeStruct((PLAN_SIZE,), I32),
        in_specs=[SMEM] * 4,
        out_specs=SMEM,
        name="plan",
    )(lengths, dest_inst, dest_slot, order)


def pack_kernel(first, items, plan, cache, up, down, held, read_sem, write_sem):
    @pl.when(lax.axis_index("inst") == INST - 1)
    def _():
        for way in range(2):

            def read(i, carry, way=way):
                code = plan[SOURCE + way * LIST + first + i]
                r = lax.shift_right_logical(code, 4)
                stored = plan[STORED + lax.bitwise_and(code, 15)]
                rows = pl.ds(pl.multiple_of(stored * BLOCK, BLOCK), BLOCK)
                pltpu.make_async_copy(
                    cache.at[:, r, rows, :], held.at[way, i], read_sem.at[way]
                ).start()
                return carry

            lax.fori_loop(0, items, read, 0)
        for way, out in enumerate((up, down)):
            pltpu.make_async_copy(held.at[way], held.at[way], read_sem.at[way]).wait()
            pltpu.make_async_copy(held.at[way], out, write_sem.at[way]).start()
        for way, out in enumerate((up, down)):
            pltpu.make_async_copy(held.at[way], out, write_sem.at[way]).wait()


def pack(first, items, plan, cache):
    shape = (items, 2, BLOCK, FEATURES)
    return pl.pallas_call(
        functools.partial(pack_kernel, first, items),
        out_shape=[jax.ShapeDtypeStruct(shape, BF16)] * 2,
        in_specs=[SMEM, HBM],
        out_specs=[HBM, HBM],
        scratch_shapes=[
            pltpu.VMEM((2, *shape), BF16),
            pltpu.SemaphoreType.DMA((2,)),
            pltpu.SemaphoreType.DMA((2,)),
        ],
        cost_estimate=pl.CostEstimate(
            flops=0, bytes_accessed=8 * items * BLOCK * FEATURES * 2, transcendentals=0
        ),
        compiler_params=params(56),
        name="pack",
    )(plan, cache)


def to_lanes(column, rows):
    shape = (rows, 128)
    same = lax.broadcasted_iota(I32, shape, 0) == lax.broadcasted_iota(I32, shape, 1)
    return jnp.sum(jnp.where(same, column, 0.0), axis=0, keepdims=True)


def to_rows(lanes, rows):
    shape = (rows, 128)
    same = lax.broadcasted_iota(I32, shape, 0) == lax.broadcasted_iota(I32, shape, 1)
    return jnp.sum(jnp.where(same, lanes, 0.0), axis=1, keepdims=True)


def project_kernel(hidden, order, gain, w_query, w_kv, out, within, lhs, stats):
    step = pl.program_id(0)

    @pl.when(step == 0)
    def _():
        row = lax.broadcasted_iota(I32, (SLOTS, 1), 0)
        scale = gain[...].astype(F32)
        sums = []
        squares = []
        for t in range(STEPS):
            x = hidden[t].astype(F32)
            sums.append(jnp.sum(x, axis=1, keepdims=True))
            squares.append(jnp.sum(x * x, axis=1, keepdims=True))
            lhs[t * SLOTS : (t + 1) * SLOTS, :] = x * scale
        lhs[24:32, :] = jnp.where(row == 0, scale, 0.0)
        sum_lanes = to_lanes(jnp.concatenate(sums, axis=0), 24)
        square_lanes = to_lanes(jnp.concatenate(squares, axis=0), 24)
        stats[...] = jnp.where(row == 1, sum_lanes, jnp.where(row == 2, square_lanes, 0.0))
        ctx = lax.axis_index("ctx")

        def search(d, carry):
            found = jnp.int32(0)
            for b in range(CTX):
                q = order[d * CTX + b]
                mine = lax.shift_right_logical(q, 4) == ctx
                found = jnp.where(mine, lax.bitwise_and(q, CTX - 1), found)
            within[d] = found
            return carry

        lax.fori_loop(0, CTX, search, 0)

    left = lhs[...].astype(BF16)
    tail = stats[...]
    row = lax.broadcasted_iota(I32, (SLOTS, 256), 0)
    wide = jnp.concatenate([tail, tail], axis=1)

    def store(o, weight):
        got = jnp.dot(left, weight, preferred_element_type=F32)
        out[o, 0:24, :] = got[0:24]
        out[o, 24:32, :] = jnp.where(row == 0, got[24:32], wide)

    @pl.when(step < 3)
    def _():
        for o in range(4):
            store(o, w_query[:, o * 256 : (o + 1) * 256])

    @pl.when(step == 3)
    def _():
        for o in range(4):
            store(o, w_kv[o // 2, :, (o % 2) * 256 : (o % 2 + 1) * 256])


def project(hidden, order, gain, w_query, w_kv):
    def whole(*shape):
        return pl.BlockSpec(shape, lambda i: (0,) * len(shape))

    return pl.pallas_call(
        project_kernel,
        out_shape=[
            jax.ShapeDtypeStruct((CTX, 32, 256), F32),
            jax.ShapeDtypeStruct((CTX,), I32),
        ],
        grid=(4,),
        in_specs=[
            whole(3, 8, 384),
            SMEM,
            whole(1, 384),
            pl.BlockSpec((384, 1024), lambda i: (0, jnp.minimum(i, 2))),
            whole(2, 384, 512),
        ],
        out_specs=[pl.BlockSpec((4, 32, 256), lambda i: (i, 0, 0)), SMEM],
        scratch_shapes=[pltpu.VMEM((32, 384), F32), pltpu.VMEM((8, 128), F32)],
        cost_estimate=pl.CostEstimate(
            flops=2 * 32 * 384 * 4096, bytes_accessed=384 * 4096 * 2, transcendentals=0
        ),
        compiler_params=params(12),
        name="project",
    )(hidden, order, gain, w_query, w_kv)


def rotate_kernel(parts, cosine, sine, out):
    total = parts[0]
    for d in range(1, CTX):
        total = total + parts[d]
    row = total[24:32]
    mean = to_rows(row[1:2, :128], 24) / MODEL_WIDTH
    square = to_rows(row[2:3, :128], 24) / MODEL_WIDTH
    scale = lax.rsqrt(square - mean * mean + NORM_EPSILON)
    value = scale * (total[0:24] - mean * row[0:1])
    for h in range(2):
        part = value[:, h * 128 : (h + 1) * 128]
        turned = part * cosine[...] + pltpu.roll(part, 64, 1) * sine[...]
        turned = turned.astype(BF16)
        for d in range(CTX):
            out[d, h] = turned


def rotate(parts, cosine, sine):
    return pl.pallas_call(
        rotate_kernel,
        out_shape=jax.ShapeDtypeStruct((CTX, 2, 24, 128), BF16),
        in_specs=[VMEM] * 3,
        out_specs=VMEM,
        compiler_params=params(8),
        name="rotate",
    )(parts, cosine, sine)


def attend(keys, values, query, position, length):
    rows = 2 * HALF_ROWS
    row = lax.broadcasted_iota(I32, (rows, 128), 0)
    high = row >= HALF_ROWS
    within = jnp.where(high, row - HALF_ROWS, row)
    group = jnp.where(high, 2, 0) + jnp.where(within >= 18, 1, 0)
    q = query.astype(F32)
    wide = jnp.concatenate([jnp.where(group == g, q, 0.0) for g in range(4)], axis=1).astype(BF16)
    score = lax.dot_general(
        wide, keys, (((1,), (1,)), ((), ())), preferred_element_type=F32
    ) * (HEAD_SIZE ** -0.5)
    line = lax.broadcasted_iota(I32, (rows, 1), 0)
    line = jnp.where(line >= HALF_ROWS, line - HALF_ROWS, line)
    visible = position <= length + lax.rem(line, STEPS)
    masked = jnp.where(visible, score, MASKED_SCORE)
    peak = jnp.max(masked, axis=1, keepdims=True)
    weight = jnp.where(visible, jnp.exp(masked - peak), 0.0)
    total = jnp.sum(weight, axis=1, keepdims=True)
    mixed = jnp.dot(weight.astype(BF16), values, preferred_element_type=F32)
    out = jnp.zeros((rows, 128), F32)
    for g in range(4):
        out = out + jnp.where(group == g, mixed[:, g * 128 : (g + 1) * 128], 0.0)
    return [
        message(
            out[h * HALF_ROWS : (h + 1) * HALF_ROWS],
            peak[h * HALF_ROWS : (h + 1) * HALF_ROWS],
            total[h * HALF_ROWS : (h + 1) * HALF_ROWS],
        )
        for h in range(2)
    ]


def message(out, peak, total):
    peak = to_lanes(peak, HALF_ROWS)
    total = to_lanes(total, HALF_ROWS)
    parts = []
    for value, count in ((peak, 3), (total, 2)):
        for _ in range(count):
            part = value.astype(BF16).astype(F32)
            parts.append(part)
            value = value - part
    row = lax.broadcasted_iota(I32, (HALF_ROWS, 128), 0)
    for i, part in enumerate(parts):
        out = jnp.where(row == STAT_ROW + i, part, out)
    return out.astype(BF16)


def blank_message():
    row = lax.broadcasted_iota(I32, (HALF_ROWS, 128), 0)
    return jnp.where(row == STAT_ROW, MASKED_SCORE, 0.0).astype(BF16)


def attend_kernel(lengths, order, cache, query, entries, new_cache, sums):
    s = pl.program_id(0)
    inst = lax.axis_index("inst")
    ctx = lax.axis_index("ctx")
    retires = inst == INST - 1
    length = lengths[inst * SLOTS + s]
    some = jnp.logical_and(
        length > 0, jnp.logical_or(retires, ctx * RANGE < length + STEPS)
    )

    @pl.when(some)
    def _():
        lane = lax.broadcasted_iota(I32, (1, RANGE), 1)
        position = jnp.zeros((1, RANGE), I32)
        for b in range(CTX):
            start = jnp.where(retires, order[ctx * CTX + b], ctx * CTX + b) * BLOCK
            position = jnp.where(
                lax.shift_right_logical(lane, 5) == b, start + lane - b * BLOCK, position
            )

        def build(b, carry):
            start = jnp.where(retires, order[ctx * CTX + b], ctx * CTX + b) * BLOCK
            rows = pl.ds(pl.multiple_of(b * BLOCK, BLOCK), BLOCK)

            @pl.when(start + BLOCK <= length)
            def _():
                new_cache[:, 0, rows, :] = cache[:, 0, rows, :]

            @pl.when(start >= length + STEPS)
            def _():
                new_cache[:, 0, rows, :] = jnp.zeros((2, BLOCK, FEATURES), BF16)

            @pl.when(jnp.logical_and(start + BLOCK > length, start < length + STEPS))
            def _():
                at = start + lax.broadcasted_iota(I32, (BLOCK, 1), 0)
                for kv in range(2):
                    block = jnp.where(at < length, cache[kv, 0, rows, :], jnp.zeros((), BF16))
                    for t in range(STEPS):
                        block = jnp.where(at == length + t, entries[0, kv, t : t + 1, :], block)
                    new_cache[kv, 0, rows, :] = block

            return carry

        lax.fori_loop(0, CTX, build, 0)
        halves = attend(new_cache[0, 0], new_cache[1, 0], query[0], position, length)
        for h in range(2):
            sums[0, h] = halves[h]

    @pl.when(jnp.logical_not(some))
    def _():
        for h in range(2):
            sums[0, h] = blank_message()

    @pl.when(jnp.logical_or(retires, jnp.logical_not(some)))
    def _():
        new_cache[...] = jnp.zeros_like(new_cache)


def attend_slots(lengths, order, cache, query, entries):
    return pl.pallas_call(
        attend_kernel,
        out_shape=[
            jax.ShapeDtypeStruct(cache.shape, BF16),
            jax.ShapeDtypeStruct((SLOTS, 2, HALF_ROWS, 128), BF16),
        ],
        grid=(SLOTS,),
        in_specs=[
            SMEM,
            SMEM,
            pl.BlockSpec((2, 1, RANGE, FEATURES), lambda s: (0, s, 0, 0)),
            pl.BlockSpec((1, 2 * HALF_ROWS, 128), lambda s: (s, 0, 0)),
            pl.BlockSpec((1, 2, 8, FEATURES), lambda s: (s, 0, 0, 0)),
        ],
        out_specs=[
            pl.BlockSpec((2, 1, RANGE, FEATURES), lambda s: (0, s, 0, 0)),
            pl.BlockSpec((1, 2, HALF_ROWS, 128), lambda s: (s, 0, 0, 0)),
        ],
        cost_estimate=pl.CostEstimate(
            flops=0, bytes_accessed=32 * 1024 * 1024, transcendentals=0
        ),
        compiler_params=params(24),
        name="attend_slots",
    )(lengths, order, cache, query, entries)


def gather_kernel(items, plan, *refs):
    count = 4 * CHUNKS - 2
    arrived, (held, sem) = refs[:count], refs[count:]
    straight = (arrived[:CHUNKS], arrived[CHUNKS : 2 * CHUNKS])
    onward = (arrived[2 * CHUNKS : 3 * CHUNKS - 1], arrived[3 * CHUNKS - 1 :])
    inst = lax.axis_index("inst")

    def fetch(way, chunk, ref, target):
        first = sum(items[:chunk])

        def one(i, carry):
            code = plan[TARGET + way * LIST + first + i]
            inside = lax.bitwise_and(code, 63)

            @pl.when(lax.shift_right_arithmetic(code, 6) == target)
            def _():
                place = lax.shift_right_logical(inside, 4)
                c = lax.bitwise_and(inside, 15)
                pltpu.make_async_copy(ref.at[i], held.at[c, place], sem.at[c, place]).start()

            return carry

        lax.fori_loop(0, items[chunk], one, 0)

    for way, target in ((0, 0), (1, 2)):

        @pl.when(inst == target)
        def _(way=way, target=target):
            for chunk in range(CHUNKS):
                fetch(way, chunk, straight[way][chunk], target)

    @pl.when(inst == 1)
    def _():
        for way in range(2):
            for chunk in range(CHUNKS - 1):
                fetch(way, chunk, onward[way][chunk], 1)

    for j in range(MOVED):

        def wait(c, carry, j=j):
            pltpu.make_async_copy(held.at[c, j], held.at[c, j], sem.at[c, j]).wait()
            return carry

        lax.fori_loop(0, plan[COUNT + j], wait, 0)


def gather(items, plan, arrived):
    return pl.pallas_call(
        functools.partial(gather_kernel, items),
        out_shape=jax.ShapeDtypeStruct((CTX, MOVED, 2, BLOCK, FEATURES), BF16),
        in_specs=[SMEM] + [ANY] * len(arrived),
        out_specs=VMEM,
        scratch_shapes=[pltpu.SemaphoreType.DMA((CTX, MOVED))],
        cost_estimate=pl.CostEstimate(flops=0, bytes_accessed=8 * 1024 * 1024, transcendentals=0),
        compiler_params=params(12),
        name="gather",
    )(plan, *arrived)


def merge_kernel(parts, out):
    blocks = [parts[d].astype(F32) for d in range(CTX)]
    peaks = []
    totals = []
    for block in blocks:
        stat = block[STAT_ROW : STAT_ROW + 8]
        peaks.append(stat[0:1] + stat[1:2] + stat[2:3])
        totals.append(stat[3:4] + stat[4:5])
    peak = functools.reduce(jnp.maximum, peaks)
    factors = [jnp.exp(p - peak) for p in peaks]
    total = functools.reduce(jnp.add, [f * t for f, t in zip(factors, totals)])
    under = to_rows(jnp.where(total > 0, total, 1.0), HALF_ROWS)
    mixed = functools.reduce(
        jnp.add, [to_rows(f, HALF_ROWS) * b for f, b in zip(factors, blocks)]
    )
    attended = (mixed / under).astype(BF16)
    for d in range(CTX):
        out[d] = attended


def merge(parts):
    return pl.pallas_call(
        merge_kernel,
        out_shape=jax.ShapeDtypeStruct(parts.shape, BF16),
        in_specs=[VMEM],
        out_specs=VMEM,
        compiler_params=params(8),
        name="merge",
    )(parts)


def place_kernel(
    plan, within, received, cache, own, by0, by1, by2, new_cache, out, held, sent, read_sem, write_sem
):
    ctx = lax.axis_index("ctx")
    for j in range(MOVED):

        @pl.when(plan[VALID + j] > 0)
        def _(j=j):
            def one(d, carry):
                rows = pl.ds(pl.multiple_of(within[d] * BLOCK, BLOCK), BLOCK)
                pltpu.make_async_copy(
                    received.at[d, j], held.at[j, :, rows, :], read_sem.at[j]
                ).start()
                return carry

            lax.fori_loop(0, CTX, one, 0)

    sent[...] = by0[...].astype(F32) + by1[...].astype(F32) + by2[...].astype(F32)
    row = lax.broadcasted_iota(I32, (SLOTS, 1), 0)
    request = jnp.full((SLOTS, 1), -1, I32)
    for s in range(SLOTS):
        request = jnp.where(row == s, plan[REQUEST + s], request)
    stays = jnp.where(lax.axis_index("inst") == INST - 1, 0.0, 1.0)
    for t in range(STEPS):
        rows = own[t * SLOTS : (t + 1) * SLOTS, 1024:].astype(F32) * stays
        for r in range(SLOTS):
            at = t * SLOTS + r
            rows = jnp.where(request == r, sent[at : at + 1, 1024:], rows)
        out[t * SLOTS : (t + 1) * SLOTS, :] = rows

    for j in range(MOVED):

        @pl.when(plan[VALID + j] > 0)
        def _(j=j):
            slot = plan[SLOT + j]
            length = plan[LENGTH + j]
            r = plan[REQUEST + slot]
            pltpu.make_async_copy(held.at[j], held.at[j], read_sem.at[j]).wait()

            def cut(b, carry):
                start = (ctx * CTX + b) * BLOCK
                rows = pl.ds(pl.multiple_of(b * BLOCK, BLOCK), BLOCK)

                @pl.when(start >= length + STEPS)
                def _():
                    held[j, :, rows, :] = jnp.zeros((2, BLOCK, FEATURES), BF16)

                @pl.when(jnp.logical_and(start + BLOCK > length, start < length + STEPS))
                def _():
                    at = start + lax.broadcasted_iota(I32, (BLOCK, 1), 0)
                    for kv in range(2):
                        block = jnp.where(at < length, held[j, kv, rows, :], jnp.zeros((), BF16))
                        for t in range(STEPS):
                            new = sent[pl.ds(t * SLOTS + r, 1), kv * 512 : (kv + 1) * 512]
                            block = jnp.where(at == length + t, new.astype(BF16), block)
                        held[j, kv, rows, :] = block

                return carry

            lax.fori_loop(0, CTX, cut, 0)
            pltpu.make_async_copy(held.at[j], new_cache.at[:, slot], write_sem.at[j]).start()

    for j in range(MOVED):

        @pl.when(plan[VALID + j] > 0)
        def _(j=j):
            pltpu.make_async_copy(
                held.at[j], new_cache.at[:, plan[SLOT + j]], write_sem.at[j]
            ).wait()


def place(plan, within, received, cache, own, by):
    return pl.pallas_call(
        place_kernel,
        out_shape=[
            jax.ShapeDtypeStruct(cache.shape, BF16),
            jax.ShapeDtypeStruct((24, 256), F32),
        ],
        in_specs=[SMEM, SMEM, ANY, HBM] + [VMEM] * 4,
        out_specs=[HBM, VMEM],
        scratch_shapes=[
            pltpu.VMEM((MOVED, 2, RANGE, FEATURES), BF16),
            pltpu.VMEM((24, 1280), F32),
            pltpu.SemaphoreType.DMA((MOVED,)),
            pltpu.SemaphoreType.DMA((MOVED,)),
        ],
        input_output_aliases={3: 0},
        compiler_params=params(12),
        name="place",
    )(plan, within, received, cache, own, *by)


def swap(x):
    return lax.all_to_all(x, "ctx", split_axis=0, concat_axis=0, tiled=True)


def after(*values):
    return lax.optimization_barrier(values)


def shards(
    cache,
    hidden,
    norm_gain,
    w_query,
    key_value_weight,
    w_out,
    lengths,
    dest_inst,
    dest_slot,
    block_order,
):
    plan = make_plan(lengths, dest_inst, dest_slot, block_order)
    operands = (
        plan, cache, hidden, norm_gain[None], w_query, key_value_weight, w_out, lengths,
        block_order,
    )
    return lax.switch(
        plan[NEED], [functools.partial(decode, items) for items in ITEMS], *operands
    )


def angles(lengths):
    own = lax.dynamic_slice_in_dim(lengths, lax.axis_index("inst") * SLOTS, SLOTS)
    token = own[None, :] + jnp.arange(STEPS, dtype=I32)[:, None]
    half = HEAD_SIZE // 2
    frequency = ROPE_BASE ** (-jnp.arange(half, dtype=F32) * 2.0 / HEAD_SIZE)
    angle = token.astype(F32).reshape(24, 1) * frequency
    is_value = lax.axis_index("ctx") >= 14
    cosine = jnp.where(is_value, 1.0, jnp.cos(angle))
    sine = jnp.where(is_value, 0.0, jnp.sin(angle))
    return jnp.concatenate([cosine, cosine], axis=1), jnp.concatenate([-sine, sine], axis=1)


def up(x):
    return lax.ppermute(x, "inst", [(INST - 1, 0)])


def down(x):
    return lax.ppermute(x, "inst", [(INST - 1, 2)])


def pass_on(from_up, from_down):
    return lax.ppermute(from_up, "inst", [(0, 1)]), lax.ppermute(from_down, "inst", [(2, 1)])


def decode(items, plan, cache, hidden, gain, w_query, w_kv, w_out, lengths, order):
    packed_up, packed_down = pack(0, items[0], plan, cache)
    up_0, down_0 = up(packed_up), down(packed_down)
    first = lax.axis_index("head") == 0
    hidden, lengths, packed_up, first = after(hidden, lengths, packed_up, first)
    cosine, sine = angles(lengths)
    projected, within = project(hidden, order, gain, w_query, w_kv)
    projected, cosine, sine, plan = after(projected, cosine, sine, plan)
    packed_up, packed_down = pack(items[0], items[1], plan, cache)
    parts, packed_up, packed_down = after(swap(projected), packed_up, packed_down)
    up_1, down_1 = up(packed_up), down(packed_down)
    turned = swap(rotate(parts, cosine, sine))
    turned = turned.reshape(32, STEPS, SLOTS, HEAD_SIZE)
    query = turned[:24].reshape(2, 12, STEPS, SLOTS, HEAD_SIZE).transpose(3, 0, 1, 2, 4)
    query = query.reshape(SLOTS, 2, 36, HEAD_SIZE)
    query = jnp.pad(query, ((0, 0), (0, 0), (0, HALF_ROWS - 36), (0, 0)))
    query = query.reshape(SLOTS, 2 * HALF_ROWS, HEAD_SIZE)
    rows = turned[24:].reshape(8, 24, HEAD_SIZE).transpose(1, 0, 2).reshape(24, 1024)
    entries = rows.reshape(STEPS, SLOTS, 2, FEATURES).transpose(1, 2, 0, 3)
    entries = jnp.pad(entries, ((0, 0), (0, 0), (0, 8 - STEPS), (0, 0)))

    new_cache, sums = attend_slots(lengths, order, cache, query, entries)
    sums, up_0, down_0 = after(sums, up_0, down_0)
    up_on, down_on = pass_on(up_0, down_0)
    attended = swap(merge(swap(sums.reshape(CTX, HALF_ROWS, HEAD_SIZE))))
    attended = attended[:, :36].reshape(SLOTS, 2, 12, STEPS, HEAD_SIZE)
    attended = attended.transpose(3, 0, 1, 2, 4).reshape(24, 24 * HEAD_SIZE)
    projected = jnp.dot(attended, w_out, preferred_element_type=F32)
    projected, up_1 = after(projected, up_1)
    held = gather(items, plan, [up_0, up_1, down_0, down_1, up_on, down_on])
    mine, other = projected[:, :192], projected[:, 192:]
    keep = jnp.where(first, mine, other)
    send_half = jnp.where(first, other, mine).astype(BF16)
    got = lax.ppermute(send_half, "head", [(0, 1), (1, 0)])
    attn_out = (keep + got.astype(F32)).astype(BF16)
    own = jnp.concatenate([rows, attn_out, jnp.zeros((24, 64), BF16)], axis=1)
    by = [lax.ppermute(own, "inst", [(INST - 1, i)]) for i in range(INST - 1)]
    *by, own, held = after(*by, own, held)
    new_cache, attn_out = place(plan, within, swap(held), new_cache, own, by)
    attn_out = attn_out[:, :192].astype(BF16)
    return new_cache, attn_out.reshape(STEPS, SLOTS, 192)


def solution(mesh):
    placed = (
        P(None, "inst", "ctx", "head"),
        P(None, "inst", "ctx"),
        P("ctx"),
        P("ctx", "head"),
        P(None, "ctx", "head"),
        P("head", "ctx"),
        P(),
        P(),
        P(),
        P(),
    )
    return jax.shard_map(
        shards,
        mesh=mesh,
        in_specs=placed,
        out_specs=(P(None, "inst", "ctx", "head"), P(None, "inst", ("ctx", "head"))),
        check_vma=False,
    )
```

```python
import functools

import jax
import jax.numpy as jnp
from jax import lax
from jax.experimental import pallas as pl
from jax.experimental.pallas import tpu as pltpu
from jax.sharding import PartitionSpec as P

MODEL_WIDTH = 6144
HEAD_SIZE = 128
ROPE_BASE = 500000.0
NORM_EPSILON = 1e-05
MASKED_SCORE = -1e30

INST = 4
CTX = 16
SLOTS = 8
STEPS = 3
MOVED = 3
BLOCK = 32
RANGE = 512
FEATURES = 512
HALF_ROWS = 48
STAT_ROW = 40
CHUNKS = 2
ITEMS = ((22, 26), (27, 31), (32, 40))
BF16 = jnp.bfloat16
F32 = jnp.float32
I32 = jnp.int32

NEW_LEN, STAYS, REQUEST = 0, 8, 16
VALID, SLOT, LENGTH, COUNT = 24, 28, 32, 36
STORED, LOGICAL = 48, 64
NEED = 80
SOURCE, TARGET = 128, 272
PLAN_SIZE = 416
LIST = 72

VMEM = pl.BlockSpec(memory_space=pltpu.VMEM)
SMEM = pl.BlockSpec(memory_space=pltpu.SMEM)
ANY = pl.BlockSpec(memory_space=pl.ANY)
HBM = pl.BlockSpec(memory_space=pltpu.HBM)


def params(mib):
    return pltpu.CompilerParams(vmem_limit_bytes=mib * 1024 * 1024)


def plan_kernel(lengths, dest_inst, dest_slot, order, plan):
    inst = lax.axis_index("inst")
    ctx = lax.axis_index("ctx")

    for s in range(SLOTS):
        own = jnp.where(inst == INST - 1, 0, lengths[inst * SLOTS + s])
        plan[NEW_LEN + s] = own
        plan[STAYS + s] = jnp.where(own > 0, 1, 0)
        plan[REQUEST + s] = -1
    for j in range(4):
        plan[VALID + j] = 0
        plan[SLOT + j] = 0
        plan[LENGTH + j] = 0
        plan[COUNT + j] = 0
    for b in range(CTX):
        q = order[ctx * CTX + b]
        plan[STORED + lax.shift_right_logical(q, 4)] = b
        plan[LOGICAL + lax.shift_right_logical(q, 4)] = q

    counts = []
    total = [jnp.int32(0)] * 3
    for r in range(SLOTS):
        long = lengths[(INST - 1) * SLOTS + r]
        count = lax.shift_right_logical(long + STEPS + RANGE - 1, 9)
        counts.append(count)
        to = dest_inst[r]
        total = [total[i] + jnp.where(to == i, count, 0) for i in range(3)]
    def weigh(part, best):
        rest = total[1] - part
        need = jnp.maximum(part + total[0], rest + total[2])
        onward = jnp.maximum(part, rest)
        size = jnp.int32(0)
        for one, two in ITEMS[:-1]:
            small = jnp.logical_or(need > one + two, onward > one)
            size = size + jnp.where(small, 1, 0)
        size = size * 256 + need + jnp.where(onward > ITEMS[-1][0], 128, 0)
        better = size < best[0]
        return jnp.where(better, size, best[0]), jnp.where(better, part, best[1])

    size, split = lax.fori_loop(0, total[1] + 1, weigh, (jnp.int32(4096), jnp.int32(0)))
    size = lax.shift_right_logical(size, 8)
    rest = total[1] - split
    plan[NEED] = size

    done = [jnp.int32(0)] * 3
    rank = [jnp.int32(0)] * 3
    for r in range(SLOTS):
        to = dest_inst[r]
        count = counts[r]
        base = jnp.where(to == 0, done[0], jnp.where(to == 1, done[1], done[2]))
        place = jnp.where(to == 0, rank[0], jnp.where(to == 1, rank[1], rank[2]))

        front = jnp.where(to == 0, split, jnp.where(to == 1, 0, LIST + rest)) + base
        back = jnp.where(to == 1, LIST + base - split, front)
        turn = split - base
        source = r * CTX
        target = to * 64 + place * CTX

        def put(c, carry, front=front, back=back, turn=turn, source=source, target=target):
            p = c + jnp.where(c < turn, front, back)
            plan[SOURCE + p] = source + c
            plan[TARGET + p] = target + c
            return carry

        lax.fori_loop(0, count, put, 0)

        @pl.when(to == inst)
        def _(r=r, place=place, count=count):
            long = lengths[(INST - 1) * SLOTS + r]
            slot = dest_slot[r]
            plan[NEW_LEN + slot] = long
            plan[STAYS + slot] = 0
            plan[REQUEST + slot] = r
            plan[VALID + place] = jnp.where(long > 0, 1, 0)
            plan[SLOT + place] = slot
            plan[LENGTH + place] = long
            plan[COUNT + place] = count

        done = [done[i] + jnp.where(to == i, count, 0) for i in range(3)]
        rank = [rank[i] + jnp.where(to == i, 1, 0) for i in range(3)]

    def clear(p, carry):
        plan[SOURCE + p] = 0
        plan[TARGET + p] = -1
        return carry

    lax.fori_loop(split + total[0], LIST, clear, 0)
    lax.fori_loop(LIST + rest + total[2], 2 * LIST, clear, 0)


def make_plan(lengths, dest_inst, dest_slot, order):
    return pl.pallas_call(
        plan_kernel,
        out_shape=jax.ShapeDtypeStruct((PLAN_SIZE,), I32),
        in_specs=[SMEM] * 4,
        out_specs=SMEM,
        name="plan",
    )(lengths, dest_inst, dest_slot, order)


def pack_kernel(first, items, plan, cache, up, down, held, read_sem, write_sem):
    @pl.when(lax.axis_index("inst") == INST - 1)
    def _():
        for way in range(2):

            def read(i, carry, way=way):
                code = plan[SOURCE + way * LIST + first + i]
                r = lax.shift_right_logical(code, 4)
                stored = plan[STORED + lax.bitwise_and(code, 15)]
                rows = pl.ds(pl.multiple_of(stored * BLOCK, BLOCK), BLOCK)
                pltpu.make_async_copy(
                    cache.at[:, r, rows, :], held.at[way, i], read_sem.at[way]
                ).start()
                return carry

            lax.fori_loop(0, items, read, 0)
        for way, out in enumerate((up, down)):
            pltpu.make_async_copy(held.at[way], held.at[way], read_sem.at[way]).wait()
            pltpu.make_async_copy(held.at[way], out, write_sem.at[way]).start()
        for way, out in enumerate((up, down)):
            pltpu.make_async_copy(held.at[way], out, write_sem.at[way]).wait()


def pack(first, items, plan, cache):
    shape = (items, 2, BLOCK, FEATURES)
    return pl.pallas_call(
        functools.partial(pack_kernel, first, items),
        out_shape=[jax.ShapeDtypeStruct(shape, BF16)] * 2,
        in_specs=[SMEM, HBM],
        out_specs=[HBM, HBM],
        scratch_shapes=[
            pltpu.VMEM((2, *shape), BF16),
            pltpu.SemaphoreType.DMA((2,)),
            pltpu.SemaphoreType.DMA((2,)),
        ],
        cost_estimate=pl.CostEstimate(
            flops=0, bytes_accessed=8 * items * BLOCK * FEATURES * 2, transcendentals=0
        ),
        compiler_params=params(56),
        name="pack",
    )(plan, cache)


def to_lanes(column, rows):
    shape = (rows, 128)
    same = lax.broadcasted_iota(I32, shape, 0) == lax.broadcasted_iota(I32, shape, 1)
    return jnp.sum(jnp.where(same, column, 0.0), axis=0, keepdims=True)


def to_rows(lanes, rows):
    shape = (rows, 128)
    same = lax.broadcasted_iota(I32, shape, 0) == lax.broadcasted_iota(I32, shape, 1)
    return jnp.sum(jnp.where(same, lanes, 0.0), axis=1, keepdims=True)


def project_kernel(hidden, order, gain, w_query, w_kv, out, within, lhs, stats):
    step = pl.program_id(0)

    @pl.when(step == 0)
    def _():
        row = lax.broadcasted_iota(I32, (SLOTS, 1), 0)
        scale = gain[...].astype(F32)
        sums = []
        squares = []
        for t in range(STEPS):
            x = hidden[t].astype(F32)
            sums.append(jnp.sum(x, axis=1, keepdims=True))
            squares.append(jnp.sum(x * x, axis=1, keepdims=True))
            lhs[t * SLOTS : (t + 1) * SLOTS, :] = x * scale
        lhs[24:32, :] = jnp.where(row == 0, scale, 0.0)
        sum_lanes = to_lanes(jnp.concatenate(sums, axis=0), 24)
        square_lanes = to_lanes(jnp.concatenate(squares, axis=0), 24)
        stats[...] = jnp.where(row == 1, sum_lanes, jnp.where(row == 2, square_lanes, 0.0))
        ctx = lax.axis_index("ctx")

        def search(d, carry):
            found = jnp.int32(0)
            for b in range(CTX):
                q = order[d * CTX + b]
                mine = lax.shift_right_logical(q, 4) == ctx
                found = jnp.where(mine, lax.bitwise_and(q, CTX - 1), found)
            within[d] = found
            return carry

        lax.fori_loop(0, CTX, search, 0)

    left = lhs[...].astype(BF16)
    tail = stats[...]
    row = lax.broadcasted_iota(I32, (SLOTS, 256), 0)
    wide = jnp.concatenate([tail, tail], axis=1)

    def store(o, weight):
        got = jnp.dot(left, weight, preferred_element_type=F32)
        out[o, 0:24, :] = got[0:24]
        out[o, 24:32, :] = jnp.where(row == 0, got[24:32], wide)

    @pl.when(step < 3)
    def _():
        for o in range(4):
            store(o, w_query[:, o * 256 : (o + 1) * 256])

    @pl.when(step == 3)
    def _():
        for o in range(4):
            store(o, w_kv[o // 2, :, (o % 2) * 256 : (o % 2 + 1) * 256])


def project(hidden, order, gain, w_query, w_kv):
    def whole(*shape):
        return pl.BlockSpec(shape, lambda i: (0,) * len(shape))

    return pl.pallas_call(
        project_kernel,
        out_shape=[
            jax.ShapeDtypeStruct((CTX, 32, 256), F32),
            jax.ShapeDtypeStruct((CTX,), I32),
        ],
        grid=(4,),
        in_specs=[
            whole(3, 8, 384),
            SMEM,
            whole(1, 384),
            pl.BlockSpec((384, 1024), lambda i: (0, jnp.minimum(i, 2))),
            whole(2, 384, 512),
        ],
        out_specs=[pl.BlockSpec((4, 32, 256), lambda i: (i, 0, 0)), SMEM],
        scratch_shapes=[pltpu.VMEM((32, 384), F32), pltpu.VMEM((8, 128), F32)],
        cost_estimate=pl.CostEstimate(
            flops=2 * 32 * 384 * 4096, bytes_accessed=384 * 4096 * 2, transcendentals=0
        ),
        compiler_params=params(12),
        name="project",
    )(hidden, order, gain, w_query, w_kv)


def rotate_kernel(parts, cosine, sine, out):
    total = parts[0]
    for d in range(1, CTX):
        total = total + parts[d]
    row = total[24:32]
    mean = to_rows(row[1:2, :128], 24) / MODEL_WIDTH
    square = to_rows(row[2:3, :128], 24) / MODEL_WIDTH
    scale = lax.rsqrt(square - mean * mean + NORM_EPSILON)
    value = scale * (total[0:24] - mean * row[0:1])
    for h in range(2):
        part = value[:, h * 128 : (h + 1) * 128]
        turned = part * cosine[...] + pltpu.roll(part, 64, 1) * sine[...]
        turned = turned.astype(BF16)
        for d in range(CTX):
            out[d, h] = turned


def rotate(parts, cosine, sine):
    return pl.pallas_call(
        rotate_kernel,
        out_shape=jax.ShapeDtypeStruct((CTX, 2, 24, 128), BF16),
        in_specs=[VMEM] * 3,
        out_specs=VMEM,
        compiler_params=params(8),
        name="rotate",
    )(parts, cosine, sine)


def attend(keys, values, query, position, length):
    rows = 2 * HALF_ROWS
    row = lax.broadcasted_iota(I32, (rows, 128), 0)
    high = row >= HALF_ROWS
    within = jnp.where(high, row - HALF_ROWS, row)
    group = jnp.where(high, 2, 0) + jnp.where(within >= 18, 1, 0)
    q = query.astype(F32)
    wide = jnp.concatenate([jnp.where(group == g, q, 0.0) for g in range(4)], axis=1).astype(BF16)
    score = lax.dot_general(
        wide, keys, (((1,), (1,)), ((), ())), preferred_element_type=F32
    ) * (HEAD_SIZE ** -0.5)
    line = lax.broadcasted_iota(I32, (rows, 1), 0)
    line = jnp.where(line >= HALF_ROWS, line - HALF_ROWS, line)
    visible = position <= length + lax.rem(line, STEPS)
    masked = jnp.where(visible, score, MASKED_SCORE)
    peak = jnp.max(masked, axis=1, keepdims=True)
    weight = jnp.where(visible, jnp.exp(masked - peak), 0.0)
    total = jnp.sum(weight, axis=1, keepdims=True)
    mixed = jnp.dot(weight.astype(BF16), values, preferred_element_type=F32)
    out = jnp.zeros((rows, 128), F32)
    for g in range(4):
        out = out + jnp.where(group == g, mixed[:, g * 128 : (g + 1) * 128], 0.0)
    return [
        message(
            out[h * HALF_ROWS : (h + 1) * HALF_ROWS],
            peak[h * HALF_ROWS : (h + 1) * HALF_ROWS],
            total[h * HALF_ROWS : (h + 1) * HALF_ROWS],
        )
        for h in range(2)
    ]


def message(out, peak, total):
    peak = to_lanes(peak, HALF_ROWS)
    total = to_lanes(total, HALF_ROWS)
    parts = []
    for value, count in ((peak, 3), (total, 2)):
        for _ in range(count):
            part = value.astype(BF16).astype(F32)
            parts.append(part)
            value = value - part
    row = lax.broadcasted_iota(I32, (HALF_ROWS, 128), 0)
    for i, part in enumerate(parts):
        out = jnp.where(row == STAT_ROW + i, part, out)
    return out.astype(BF16)


def blank_message():
    row = lax.broadcasted_iota(I32, (HALF_ROWS, 128), 0)
    return jnp.where(row == STAT_ROW, MASKED_SCORE, 0.0).astype(BF16)


def attend_kernel(lengths, order, cache, query, entries, new_cache, sums):
    s = pl.program_id(0)
    inst = lax.axis_index("inst")
    ctx = lax.axis_index("ctx")
    retires = inst == INST - 1
    length = lengths[inst * SLOTS + s]
    some = jnp.logical_and(
        length > 0, jnp.logical_or(retires, ctx * RANGE < length + STEPS)
    )

    @pl.when(some)
    def _():
        lane = lax.broadcasted_iota(I32, (1, RANGE), 1)
        position = jnp.zeros((1, RANGE), I32)
        for b in range(CTX):
            start = jnp.where(retires, order[ctx * CTX + b], ctx * CTX + b) * BLOCK
            position = jnp.where(
                lax.shift_right_logical(lane, 5) == b, start + lane - b * BLOCK, position
            )

        new_cache[...] = cache[...]

        def build(b, carry):
            start = jnp.where(retires, order[ctx * CTX + b], ctx * CTX + b) * BLOCK
            rows = pl.ds(pl.multiple_of(b * BLOCK, BLOCK), BLOCK)

            @pl.when(jnp.logical_and(start >= length + STEPS, jnp.logical_not(retires)))
            def _():
                new_cache[:, 0, rows, :] = jnp.zeros((2, BLOCK, FEATURES), BF16)

            @pl.when(jnp.logical_and(start + BLOCK > length, start < length + STEPS))
            def _():
                at = start + lax.broadcasted_iota(I32, (BLOCK, 1), 0)
                for kv in range(2):
                    block = jnp.where(at < length, cache[kv, 0, rows, :], jnp.zeros((), BF16))
                    for t in range(STEPS):
                        block = jnp.where(at == length + t, entries[0, kv, t : t + 1, :], block)
                    new_cache[kv, 0, rows, :] = block

            return carry

        whole = jnp.logical_and(jnp.logical_not(retires), (ctx + 1) * RANGE <= length)
        lax.fori_loop(0, jnp.where(whole, 0, CTX), build, 0)
        halves = attend(new_cache[0, 0], new_cache[1, 0], query[0], position, length)
        for h in range(2):
            sums[0, h] = halves[h]

    @pl.when(jnp.logical_not(some))
    def _():
        for h in range(2):
            sums[0, h] = blank_message()

    @pl.when(jnp.logical_or(retires, jnp.logical_not(some)))
    def _():
        new_cache[...] = jnp.zeros_like(new_cache)


def attend_slots(lengths, order, cache, query, entries):
    return pl.pallas_call(
        attend_kernel,
        out_shape=[
            jax.ShapeDtypeStruct(cache.shape, BF16),
            jax.ShapeDtypeStruct((SLOTS, 2, HALF_ROWS, 128), BF16),
        ],
        grid=(SLOTS,),
        in_specs=[
            SMEM,
            SMEM,
            pl.BlockSpec((2, 1, RANGE, FEATURES), lambda s: (0, s, 0, 0)),
            pl.BlockSpec((1, 2 * HALF_ROWS, 128), lambda s: (s, 0, 0)),
            pl.BlockSpec((1, 2, 8, FEATURES), lambda s: (s, 0, 0, 0)),
        ],
        out_specs=[
            pl.BlockSpec((2, 1, RANGE, FEATURES), lambda s: (0, s, 0, 0)),
            pl.BlockSpec((1, 2, HALF_ROWS, 128), lambda s: (s, 0, 0, 0)),
        ],
        cost_estimate=pl.CostEstimate(
            flops=0, bytes_accessed=32 * 1024 * 1024, transcendentals=0
        ),
        compiler_params=params(24),
        name="attend_slots",
    )(lengths, order, cache, query, entries)


def gather_kernel(items, plan, *refs):
    count = 4 * CHUNKS - 2
    arrived, (held, sem) = refs[:count], refs[count:]
    straight = (arrived[:CHUNKS], arrived[CHUNKS : 2 * CHUNKS])
    onward = (arrived[2 * CHUNKS : 3 * CHUNKS - 1], arrived[3 * CHUNKS - 1 :])
    inst = lax.axis_index("inst")

    def fetch(way, chunk, ref, target):
        first = sum(items[:chunk])

        def one(i, carry):
            code = plan[TARGET + way * LIST + first + i]
            inside = lax.bitwise_and(code, 63)

            @pl.when(lax.shift_right_arithmetic(code, 6) == target)
            def _():
                place = lax.shift_right_logical(inside, 4)
                c = lax.bitwise_and(inside, 15)
                pltpu.make_async_copy(ref.at[i], held.at[c, place], sem.at[c, place]).start()

            return carry

        lax.fori_loop(0, items[chunk], one, 0)

    for way, target in ((0, 0), (1, 2)):

        @pl.when(inst == target)
        def _(way=way, target=target):
            for chunk in range(CHUNKS):
                fetch(way, chunk, straight[way][chunk], target)

    @pl.when(inst == 1)
    def _():
        for way in range(2):
            for chunk in range(CHUNKS - 1):
                fetch(way, chunk, onward[way][chunk], 1)

    for j in range(MOVED):

        def wait(c, carry, j=j):
            pltpu.make_async_copy(held.at[c, j], held.at[c, j], sem.at[c, j]).wait()
            return carry

        lax.fori_loop(0, plan[COUNT + j], wait, 0)


def gather(items, plan, arrived):
    return pl.pallas_call(
        functools.partial(gather_kernel, items),
        out_shape=jax.ShapeDtypeStruct((CTX, MOVED, 2, BLOCK, FEATURES), BF16),
        in_specs=[SMEM] + [ANY] * len(arrived),
        out_specs=VMEM,
        scratch_shapes=[pltpu.SemaphoreType.DMA((CTX, MOVED))],
        cost_estimate=pl.CostEstimate(flops=0, bytes_accessed=8 * 1024 * 1024, transcendentals=0),
        compiler_params=params(12),
        name="gather",
    )(plan, *arrived)


def merge_kernel(parts, out):
    blocks = [parts[d].astype(F32) for d in range(CTX)]
    peaks = []
    totals = []
    for block in blocks:
        stat = block[STAT_ROW : STAT_ROW + 8]
        peaks.append(stat[0:1] + stat[1:2] + stat[2:3])
        totals.append(stat[3:4] + stat[4:5])
    peak = functools.reduce(jnp.maximum, peaks)
    factors = [jnp.exp(p - peak) for p in peaks]
    total = functools.reduce(jnp.add, [f * t for f, t in zip(factors, totals)])
    under = to_rows(jnp.where(total > 0, total, 1.0), HALF_ROWS)
    mixed = functools.reduce(
        jnp.add, [to_rows(f, HALF_ROWS) * b for f, b in zip(factors, blocks)]
    )
    attended = (mixed / under).astype(BF16)
    for d in range(CTX):
        out[d] = attended


def merge(parts):
    return pl.pallas_call(
        merge_kernel,
        out_shape=jax.ShapeDtypeStruct(parts.shape, BF16),
        in_specs=[VMEM],
        out_specs=VMEM,
        compiler_params=params(8),
        name="merge",
    )(parts)


def place_kernel(
    plan, within, received, cache, own, by0, by1, by2, new_cache, out, fixed, empty, sent, sem
):
    ctx = lax.axis_index("ctx")
    empty[...] = jnp.zeros_like(empty)
    sent[...] = by0[...].astype(F32) + by1[...].astype(F32) + by2[...].astype(F32)
    row = lax.broadcasted_iota(I32, (SLOTS, 1), 0)
    request = jnp.full((SLOTS, 1), -1, I32)
    for s in range(SLOTS):
        request = jnp.where(row == s, plan[REQUEST + s], request)
    stays = jnp.where(lax.axis_index("inst") == INST - 1, 0.0, 1.0)
    for t in range(STEPS):
        rows = own[t * SLOTS : (t + 1) * SLOTS, 1024:].astype(F32) * stays
        for r in range(SLOTS):
            at = t * SLOTS + r
            rows = jnp.where(request == r, sent[at : at + 1, 1024:], rows)
        out[t * SLOTS : (t + 1) * SLOTS, :] = rows

    for j in range(MOVED):

        @pl.when(plan[VALID + j] > 0)
        def _(j=j):
            slot = plan[SLOT + j]
            length = plan[LENGTH + j]
            r = plan[REQUEST + slot]

            def one(d, carry):
                b = within[d]
                start = (ctx * CTX + b) * BLOCK
                rows = pl.ds(pl.multiple_of(b * BLOCK, BLOCK), BLOCK)
                target = new_cache.at[:, slot, rows, :]

                @pl.when(start + BLOCK <= length)
                def _():
                    pltpu.make_async_copy(received.at[d, j], target, sem.at[j]).start()

                @pl.when(start >= length + STEPS)
                def _():
                    pltpu.make_async_copy(empty, target, sem.at[j]).start()

                @pl.when(jnp.logical_and(start + BLOCK > length, start < length + STEPS))
                def _():
                    at = start + lax.broadcasted_iota(I32, (BLOCK, 1), 0)
                    half = lax.bitwise_and(b, 1)
                    for kv in range(2):
                        block = jnp.where(at < length, received[d, j, kv], jnp.zeros((), BF16))
                        for t in range(STEPS):
                            new = sent[pl.ds(t * SLOTS + r, 1), kv * 512 : (kv + 1) * 512]
                            block = jnp.where(at == length + t, new.astype(BF16), block)
                        fixed[j, half, kv] = block
                    pltpu.make_async_copy(fixed.at[j, half], target, sem.at[j]).start()

                return carry

            lax.fori_loop(0, CTX, one, 0)

    for j in range(MOVED):

        @pl.when(plan[VALID + j] > 0)
        def _(j=j):
            whole = new_cache.at[:, plan[SLOT + j]]
            pltpu.make_async_copy(whole, whole, sem.at[j]).wait()


def place(plan, within, received, cache, own, by):
    return pl.pallas_call(
        place_kernel,
        out_shape=[
            jax.ShapeDtypeStruct(cache.shape, BF16),
            jax.ShapeDtypeStruct((24, 256), F32),
        ],
        in_specs=[SMEM, SMEM, VMEM, HBM] + [VMEM] * 4,
        out_specs=[HBM, VMEM],
        scratch_shapes=[
            pltpu.VMEM((MOVED, 2, 2, BLOCK, FEATURES), BF16),
            pltpu.VMEM((2, BLOCK, FEATURES), BF16),
            pltpu.VMEM((24, 1280), F32),
            pltpu.SemaphoreType.DMA((MOVED,)),
        ],
        input_output_aliases={3: 0},
        compiler_params=params(12),
        name="place",
    )(plan, within, received, cache, own, *by)


def swap(x):
    return lax.all_to_all(x, "ctx", split_axis=0, concat_axis=0, tiled=True)


def after(*values):
    return lax.optimization_barrier(values)


def shards(
    cache,
    hidden,
    norm_gain,
    w_query,
    key_value_weight,
    w_out,
    lengths,
    dest_inst,
    dest_slot,
    block_order,
):
    plan = make_plan(lengths, dest_inst, dest_slot, block_order)
    operands = (
        plan, cache, hidden, norm_gain[None], w_query, key_value_weight, w_out, lengths,
        block_order,
    )
    return lax.switch(
        plan[NEED], [functools.partial(decode, items) for items in ITEMS], *operands
    )


def angles(lengths):
    own = lax.dynamic_slice_in_dim(lengths, lax.axis_index("inst") * SLOTS, SLOTS)
    token = own[None, :] + jnp.arange(STEPS, dtype=I32)[:, None]
    half = HEAD_SIZE // 2
    frequency = ROPE_BASE ** (-jnp.arange(half, dtype=F32) * 2.0 / HEAD_SIZE)
    angle = token.astype(F32).reshape(24, 1) * frequency
    is_value = lax.axis_index("ctx") >= 14
    cosine = jnp.where(is_value, 1.0, jnp.cos(angle))
    sine = jnp.where(is_value, 0.0, jnp.sin(angle))
    return jnp.concatenate([cosine, cosine], axis=1), jnp.concatenate([-sine, sine], axis=1)


def up(x):
    return lax.ppermute(x, "inst", [(INST - 1, 0)])


def down(x):
    return lax.ppermute(x, "inst", [(INST - 1, 2)])


def pass_on(from_up, from_down):
    return lax.ppermute(from_up, "inst", [(0, 1)]), lax.ppermute(from_down, "inst", [(2, 1)])


def decode(items, plan, cache, hidden, gain, w_query, w_kv, w_out, lengths, order):
    packed_up, packed_down = pack(0, items[0], plan, cache)
    up_0, down_0 = up(packed_up), down(packed_down)
    first = lax.axis_index("head") == 0
    hidden, lengths, packed_up, first = after(hidden, lengths, packed_up, first)
    cosine, sine = angles(lengths)
    projected, within = project(hidden, order, gain, w_query, w_kv)
    projected, cosine, sine, plan = after(projected, cosine, sine, plan)
    packed_up, packed_down = pack(items[0], items[1], plan, cache)
    parts, packed_up, packed_down = after(swap(projected), packed_up, packed_down)
    up_1, down_1 = up(packed_up), down(packed_down)
    turned = swap(rotate(parts, cosine, sine))
    turned = turned.reshape(32, STEPS, SLOTS, HEAD_SIZE)
    query = turned[:24].reshape(2, 12, STEPS, SLOTS, HEAD_SIZE).transpose(3, 0, 1, 2, 4)
    query = query.reshape(SLOTS, 2, 36, HEAD_SIZE)
    query = jnp.pad(query, ((0, 0), (0, 0), (0, HALF_ROWS - 36), (0, 0)))
    query = query.reshape(SLOTS, 2 * HALF_ROWS, HEAD_SIZE)
    rows = turned[24:].reshape(8, 24, HEAD_SIZE).transpose(1, 0, 2).reshape(24, 1024)
    entries = rows.reshape(STEPS, SLOTS, 2, FEATURES).transpose(1, 2, 0, 3)
    entries = jnp.pad(entries, ((0, 0), (0, 0), (0, 8 - STEPS), (0, 0)))

    new_cache, sums = attend_slots(lengths, order, cache, query, entries)
    sums, up_0, down_0 = after(sums, up_0, down_0)
    up_on, down_on = pass_on(up_0, down_0)
    attended = swap(merge(swap(sums.reshape(CTX, HALF_ROWS, HEAD_SIZE))))
    attended = attended[:, :36].reshape(SLOTS, 2, 12, STEPS, HEAD_SIZE)
    attended = attended.transpose(3, 0, 1, 2, 4).reshape(24, 24 * HEAD_SIZE)
    projected = jnp.dot(attended, w_out, preferred_element_type=F32)
    projected, up_1 = after(projected, up_1)
    held = gather(items, plan, [up_0, up_1, down_0, down_1, up_on, down_on])
    mine, other = projected[:, :192], projected[:, 192:]
    keep = jnp.where(first, mine, other)
    send_half = jnp.where(first, other, mine).astype(BF16)
    got = lax.ppermute(send_half, "head", [(0, 1), (1, 0)])
    attn_out = (keep + got.astype(F32)).astype(BF16)
    own = jnp.concatenate([rows, attn_out, jnp.zeros((24, 64), BF16)], axis=1)
    by = [lax.ppermute(own, "inst", [(INST - 1, i)]) for i in range(INST - 1)]
    *by, own, held = after(*by, own, held)
    new_cache, attn_out = place(plan, within, swap(held), new_cache, own, by)
    attn_out = attn_out[:, :192].astype(BF16)
    return new_cache, attn_out.reshape(STEPS, SLOTS, 192)


def solution(mesh):
    placed = (
        P(None, "inst", "ctx", "head"),
        P(None, "inst", "ctx"),
        P("ctx"),
        P("ctx", "head"),
        P(None, "ctx", "head"),
        P("head", "ctx"),
        P(),
        P(),
        P(),
        P(),
    )
    return jax.shard_map(
        shards,
        mesh=mesh,
        in_specs=placed,
        out_specs=(P(None, "inst", "ctx", "head"), P(None, "inst", ("ctx", "head"))),
        check_vma=False,
    )
```

```python
import functools

import jax
import jax.numpy as jnp
from jax import lax
from jax.experimental import pallas as pl
from jax.experimental.pallas import tpu as pltpu
from jax.sharding import PartitionSpec as P

MODEL_WIDTH = 6144
HEAD_SIZE = 128
ROPE_BASE = 500000.0
NORM_EPSILON = 1e-05
MASKED_SCORE = -1e30

INST = 4
CTX = 16
SLOTS = 8
STEPS = 3
MOVED = 3
BLOCK = 32
RANGE = 512
FEATURES = 512
HALF_ROWS = 48
STAT_ROW = 40
CHUNKS = 2
ITEMS = ((22, 26), (27, 31), (32, 40))
BF16 = jnp.bfloat16
F32 = jnp.float32
I32 = jnp.int32

NEW_LEN, STAYS, REQUEST = 0, 8, 16
VALID, SLOT, LENGTH, COUNT = 24, 28, 32, 36
STORED, LOGICAL = 48, 64
NEED = 80
SOURCE, TARGET = 128, 272
PLAN_SIZE = 416
LIST = 72

VMEM = pl.BlockSpec(memory_space=pltpu.VMEM)
SMEM = pl.BlockSpec(memory_space=pltpu.SMEM)
ANY = pl.BlockSpec(memory_space=pl.ANY)
HBM = pl.BlockSpec(memory_space=pltpu.HBM)


def params(mib):
    return pltpu.CompilerParams(vmem_limit_bytes=mib * 1024 * 1024)


def plan_kernel(lengths, dest_inst, dest_slot, order, plan):
    inst = lax.axis_index("inst")
    ctx = lax.axis_index("ctx")

    for s in range(SLOTS):
        own = jnp.where(inst == INST - 1, 0, lengths[inst * SLOTS + s])
        plan[NEW_LEN + s] = own
        plan[STAYS + s] = jnp.where(own > 0, 1, 0)
        plan[REQUEST + s] = -1
    for j in range(4):
        plan[VALID + j] = 0
        plan[SLOT + j] = 0
        plan[LENGTH + j] = 0
        plan[COUNT + j] = 0
    for b in range(CTX):
        q = order[ctx * CTX + b]
        plan[STORED + lax.shift_right_logical(q, 4)] = b
        plan[LOGICAL + lax.shift_right_logical(q, 4)] = q

    counts = []
    total = [jnp.int32(0)] * 3
    for r in range(SLOTS):
        long = lengths[(INST - 1) * SLOTS + r]
        count = lax.shift_right_logical(long + STEPS + RANGE - 1, 9)
        counts.append(count)
        to = dest_inst[r]
        total = [total[i] + jnp.where(to == i, count, 0) for i in range(3)]
    def weigh(part, best):
        rest = total[1] - part
        need = jnp.maximum(part + total[0], rest + total[2])
        onward = jnp.maximum(part, rest)
        size = jnp.int32(0)
        for one, two in ITEMS[:-1]:
            small = jnp.logical_or(need > one + two, onward > one)
            size = size + jnp.where(small, 1, 0)
        size = size * 256 + need + jnp.where(onward > ITEMS[-1][0], 128, 0)
        better = size < best[0]
        return jnp.where(better, size, best[0]), jnp.where(better, part, best[1])

    size, split = lax.fori_loop(0, total[1] + 1, weigh, (jnp.int32(4096), jnp.int32(0)))
    size = lax.shift_right_logical(size, 8)
    rest = total[1] - split
    plan[NEED] = size

    done = [jnp.int32(0)] * 3
    rank = [jnp.int32(0)] * 3
    for r in range(SLOTS):
        to = dest_inst[r]
        count = counts[r]
        base = jnp.where(to == 0, done[0], jnp.where(to == 1, done[1], done[2]))
        place = jnp.where(to == 0, rank[0], jnp.where(to == 1, rank[1], rank[2]))

        front = jnp.where(to == 0, split, jnp.where(to == 1, 0, LIST + rest)) + base
        back = jnp.where(to == 1, LIST + base - split, front)
        turn = split - base
        source = r * CTX
        target = to * 64 + place * CTX

        def put(c, carry, front=front, back=back, turn=turn, source=source, target=target):
            p = c + jnp.where(c < turn, front, back)
            plan[SOURCE + p] = source + c
            plan[TARGET + p] = target + c
            return carry

        lax.fori_loop(0, count, put, 0)

        @pl.when(to == inst)
        def _(r=r, place=place, count=count):
            long = lengths[(INST - 1) * SLOTS + r]
            slot = dest_slot[r]
            plan[NEW_LEN + slot] = long
            plan[STAYS + slot] = 0
            plan[REQUEST + slot] = r
            plan[VALID + place] = jnp.where(long > 0, 1, 0)
            plan[SLOT + place] = slot
            plan[LENGTH + place] = long
            plan[COUNT + place] = count

        done = [done[i] + jnp.where(to == i, count, 0) for i in range(3)]
        rank = [rank[i] + jnp.where(to == i, 1, 0) for i in range(3)]

    def clear(p, carry):
        plan[SOURCE + p] = 0
        plan[TARGET + p] = -1
        return carry

    lax.fori_loop(split + total[0], LIST, clear, 0)
    lax.fori_loop(LIST + rest + total[2], 2 * LIST, clear, 0)


def make_plan(lengths, dest_inst, dest_slot, order):
    return pl.pallas_call(
        plan_kernel,
        out_shape=jax.ShapeDtypeStruct((PLAN_SIZE,), I32),
        in_specs=[SMEM] * 4,
        out_specs=SMEM,
        name="plan",
    )(lengths, dest_inst, dest_slot, order)


def pack_kernel(first, items, plan, cache, up, down, held, read_sem, write_sem):
    @pl.when(lax.axis_index("inst") == INST - 1)
    def _():
        for way in range(2):

            def read(i, carry, way=way):
                code = plan[SOURCE + way * LIST + first + i]
                r = lax.shift_right_logical(code, 4)
                stored = plan[STORED + lax.bitwise_and(code, 15)]
                rows = pl.ds(pl.multiple_of(stored * BLOCK, BLOCK), BLOCK)
                pltpu.make_async_copy(
                    cache.at[:, r, rows, :], held.at[way, i], read_sem.at[way]
                ).start()
                return carry

            lax.fori_loop(0, items, read, 0)
        for way, out in enumerate((up, down)):
            pltpu.make_async_copy(held.at[way], held.at[way], read_sem.at[way]).wait()
            pltpu.make_async_copy(held.at[way], out, write_sem.at[way]).start()
        for way, out in enumerate((up, down)):
            pltpu.make_async_copy(held.at[way], out, write_sem.at[way]).wait()


def pack(first, items, plan, cache):
    shape = (items, 2, BLOCK, FEATURES)
    return pl.pallas_call(
        functools.partial(pack_kernel, first, items),
        out_shape=[jax.ShapeDtypeStruct(shape, BF16)] * 2,
        in_specs=[SMEM, HBM],
        out_specs=[HBM, HBM],
        scratch_shapes=[
            pltpu.VMEM((2, *shape), BF16),
            pltpu.SemaphoreType.DMA((2,)),
            pltpu.SemaphoreType.DMA((2,)),
        ],
        cost_estimate=pl.CostEstimate(
            flops=0, bytes_accessed=8 * items * BLOCK * FEATURES * 2, transcendentals=0
        ),
        compiler_params=params(56),
        name="pack",
    )(plan, cache)


def to_lanes(column, rows):
    shape = (rows, 128)
    same = lax.broadcasted_iota(I32, shape, 0) == lax.broadcasted_iota(I32, shape, 1)
    return jnp.sum(jnp.where(same, column, 0.0), axis=0, keepdims=True)


def to_rows(lanes, rows):
    shape = (rows, 128)
    same = lax.broadcasted_iota(I32, shape, 0) == lax.broadcasted_iota(I32, shape, 1)
    return jnp.sum(jnp.where(same, lanes, 0.0), axis=1, keepdims=True)


def project_kernel(hidden, order, gain, w_query, w_kv, out, within, lhs, stats):
    step = pl.program_id(0)

    @pl.when(step == 0)
    def _():
        row = lax.broadcasted_iota(I32, (SLOTS, 1), 0)
        scale = gain[...].astype(F32)
        sums = []
        squares = []
        for t in range(STEPS):
            x = hidden[t].astype(F32)
            sums.append(jnp.sum(x, axis=1, keepdims=True))
            squares.append(jnp.sum(x * x, axis=1, keepdims=True))
            lhs[t * SLOTS : (t + 1) * SLOTS, :] = x * scale
        lhs[24:32, :] = jnp.where(row == 0, scale, 0.0)
        sum_lanes = to_lanes(jnp.concatenate(sums, axis=0), 24)
        square_lanes = to_lanes(jnp.concatenate(squares, axis=0), 24)
        stats[...] = jnp.where(row == 1, sum_lanes, jnp.where(row == 2, square_lanes, 0.0))
        ctx = lax.axis_index("ctx")

        def search(d, carry):
            found = jnp.int32(0)
            for b in range(CTX):
                q = order[d * CTX + b]
                mine = lax.shift_right_logical(q, 4) == ctx
                found = jnp.where(mine, lax.bitwise_and(q, CTX - 1), found)
            within[d] = found
            return carry

        lax.fori_loop(0, CTX, search, 0)

    left = lhs[...].astype(BF16)
    tail = stats[...]
    row = lax.broadcasted_iota(I32, (SLOTS, 256), 0)
    wide = jnp.concatenate([tail, tail], axis=1)

    def store(o, weight):
        got = jnp.dot(left, weight, preferred_element_type=F32)
        out[o, 0:24, :] = got[0:24]
        out[o, 24:32, :] = jnp.where(row == 0, got[24:32], wide)

    @pl.when(step < 3)
    def _():
        for o in range(4):
            store(o, w_query[:, o * 256 : (o + 1) * 256])

    @pl.when(step == 3)
    def _():
        for o in range(4):
            store(o, w_kv[o // 2, :, (o % 2) * 256 : (o % 2 + 1) * 256])


def project(hidden, order, gain, w_query, w_kv):
    def whole(*shape):
        return pl.BlockSpec(shape, lambda i: (0,) * len(shape))

    return pl.pallas_call(
        project_kernel,
        out_shape=[
            jax.ShapeDtypeStruct((CTX, 32, 256), F32),
            jax.ShapeDtypeStruct((CTX,), I32),
        ],
        grid=(4,),
        in_specs=[
            whole(3, 8, 384),
            SMEM,
            whole(1, 384),
            pl.BlockSpec((384, 1024), lambda i: (0, jnp.minimum(i, 2))),
            whole(2, 384, 512),
        ],
        out_specs=[pl.BlockSpec((4, 32, 256), lambda i: (i, 0, 0)), SMEM],
        scratch_shapes=[pltpu.VMEM((32, 384), F32), pltpu.VMEM((8, 128), F32)],
        cost_estimate=pl.CostEstimate(
            flops=2 * 32 * 384 * 4096, bytes_accessed=384 * 4096 * 2, transcendentals=0
        ),
        compiler_params=params(12),
        name="project",
    )(hidden, order, gain, w_query, w_kv)


def rotate_kernel(parts, cosine, sine, out):
    total = parts[0]
    for d in range(1, CTX):
        total = total + parts[d]
    row = total[24:32]
    mean = to_rows(row[1:2, :128], 24) / MODEL_WIDTH
    square = to_rows(row[2:3, :128], 24) / MODEL_WIDTH
    scale = lax.rsqrt(square - mean * mean + NORM_EPSILON)
    value = scale * (total[0:24] - mean * row[0:1])
    for h in range(2):
        part = value[:, h * 128 : (h + 1) * 128]
        turned = part * cosine[...] + pltpu.roll(part, 64, 1) * sine[...]
        turned = turned.astype(BF16)
        for d in range(CTX):
            out[d, h] = turned


def rotate(parts, cosine, sine):
    return pl.pallas_call(
        rotate_kernel,
        out_shape=jax.ShapeDtypeStruct((CTX, 2, 24, 128), BF16),
        in_specs=[VMEM] * 3,
        out_specs=VMEM,
        compiler_params=params(8),
        name="rotate",
    )(parts, cosine, sine)


def attend(keys, values, query, position, length):
    rows = 2 * HALF_ROWS
    row = lax.broadcasted_iota(I32, (rows, 128), 0)
    high = row >= HALF_ROWS
    within = jnp.where(high, row - HALF_ROWS, row)
    group = jnp.where(high, 2, 0) + jnp.where(within >= 18, 1, 0)
    q = query.astype(F32)
    wide = jnp.concatenate([jnp.where(group == g, q, 0.0) for g in range(4)], axis=1).astype(BF16)
    score = lax.dot_general(
        wide, keys, (((1,), (1,)), ((), ())), preferred_element_type=F32
    ) * (HEAD_SIZE ** -0.5)
    line = lax.broadcasted_iota(I32, (rows, 1), 0)
    line = jnp.where(line >= HALF_ROWS, line - HALF_ROWS, line)
    visible = position <= length + lax.rem(line, STEPS)
    masked = jnp.where(visible, score, MASKED_SCORE)
    peak = jnp.max(masked, axis=1, keepdims=True)
    weight = jnp.where(visible, jnp.exp(masked - peak), 0.0)
    total = jnp.sum(weight, axis=1, keepdims=True)
    mixed = jnp.dot(weight.astype(BF16), values, preferred_element_type=F32)
    out = jnp.zeros((rows, 128), F32)
    for g in range(4):
        out = out + jnp.where(group == g, mixed[:, g * 128 : (g + 1) * 128], 0.0)
    return [
        message(
            out[h * HALF_ROWS : (h + 1) * HALF_ROWS],
            peak[h * HALF_ROWS : (h + 1) * HALF_ROWS],
            total[h * HALF_ROWS : (h + 1) * HALF_ROWS],
        )
        for h in range(2)
    ]


def message(out, peak, total):
    peak = to_lanes(peak, HALF_ROWS)
    total = to_lanes(total, HALF_ROWS)
    parts = []
    for value, count in ((peak, 3), (total, 2)):
        for _ in range(count):
            part = value.astype(BF16).astype(F32)
            parts.append(part)
            value = value - part
    row = lax.broadcasted_iota(I32, (HALF_ROWS, 128), 0)
    for i, part in enumerate(parts):
        out = jnp.where(row == STAT_ROW + i, part, out)
    return out.astype(BF16)


def blank_message():
    row = lax.broadcasted_iota(I32, (HALF_ROWS, 128), 0)
    return jnp.where(row == STAT_ROW, MASKED_SCORE, 0.0).astype(BF16)


def attend_kernel(lengths, order, cache, query, entries, new_cache, sums):
    s = pl.program_id(0)
    inst = lax.axis_index("inst")
    ctx = lax.axis_index("ctx")
    retires = inst == INST - 1
    length = lengths[inst * SLOTS + s]
    some = jnp.logical_and(
        length > 0, jnp.logical_or(retires, ctx * RANGE < length + STEPS)
    )

    @pl.when(some)
    def _():
        lane = lax.broadcasted_iota(I32, (1, RANGE), 1)
        position = jnp.zeros((1, RANGE), I32)
        for b in range(CTX):
            start = jnp.where(retires, order[ctx * CTX + b], ctx * CTX + b) * BLOCK
            position = jnp.where(
                lax.shift_right_logical(lane, 5) == b, start + lane - b * BLOCK, position
            )

        def meets(b, found):
            start = order[ctx * CTX + b] * BLOCK
            here = jnp.logical_and(start + BLOCK > length, start < length + STEPS)
            return jnp.where(here, 1, found)

        found = lax.fori_loop(0, jnp.where(retires, CTX, 0), meets, jnp.int32(0))
        direct = jnp.logical_and(retires, found == 0)

        def finish(keys, values):
            halves = attend(keys, values, query[0], position, length)
            for h in range(2):
                sums[0, h] = halves[h]

        @pl.when(direct)
        def _():
            finish(cache[0, 0], cache[1, 0])

        @pl.when(jnp.logical_not(direct))
        def _():
            new_cache[...] = cache[...]

            def build(b, carry):
                start = jnp.where(retires, order[ctx * CTX + b], ctx * CTX + b) * BLOCK
                rows = pl.ds(pl.multiple_of(b * BLOCK, BLOCK), BLOCK)

                @pl.when(jnp.logical_and(start >= length + STEPS, jnp.logical_not(retires)))
                def _():
                    new_cache[:, 0, rows, :] = jnp.zeros((2, BLOCK, FEATURES), BF16)

                @pl.when(jnp.logical_and(start + BLOCK > length, start < length + STEPS))
                def _():
                    at = start + lax.broadcasted_iota(I32, (BLOCK, 1), 0)
                    for kv in range(2):
                        block = jnp.where(at < length, cache[kv, 0, rows, :], jnp.zeros((), BF16))
                        for t in range(STEPS):
                            block = jnp.where(at == length + t, entries[0, kv, t : t + 1, :], block)
                        new_cache[kv, 0, rows, :] = block

                return carry

            whole = jnp.logical_and(jnp.logical_not(retires), (ctx + 1) * RANGE <= length)
            lax.fori_loop(0, jnp.where(whole, 0, CTX), build, 0)
            finish(new_cache[0, 0], new_cache[1, 0])

    @pl.when(jnp.logical_not(some))
    def _():
        for h in range(2):
            sums[0, h] = blank_message()

    @pl.when(jnp.logical_or(retires, jnp.logical_not(some)))
    def _():
        new_cache[...] = jnp.zeros_like(new_cache)


def attend_slots(lengths, order, cache, query, entries):
    return pl.pallas_call(
        attend_kernel,
        out_shape=[
            jax.ShapeDtypeStruct(cache.shape, BF16),
            jax.ShapeDtypeStruct((SLOTS, 2, HALF_ROWS, 128), BF16),
        ],
        grid=(SLOTS,),
        in_specs=[
            SMEM,
            SMEM,
            pl.BlockSpec((2, 1, RANGE, FEATURES), lambda s: (0, s, 0, 0)),
            pl.BlockSpec((1, 2 * HALF_ROWS, 128), lambda s: (s, 0, 0)),
            pl.BlockSpec((1, 2, 8, FEATURES), lambda s: (s, 0, 0, 0)),
        ],
        out_specs=[
            pl.BlockSpec((2, 1, RANGE, FEATURES), lambda s: (0, s, 0, 0)),
            pl.BlockSpec((1, 2, HALF_ROWS, 128), lambda s: (s, 0, 0, 0)),
        ],
        cost_estimate=pl.CostEstimate(
            flops=0, bytes_accessed=32 * 1024 * 1024, transcendentals=0
        ),
        compiler_params=params(24),
        name="attend_slots",
    )(lengths, order, cache, query, entries)


def gather_kernel(items, plan, *refs):
    count = 4 * CHUNKS - 2
    arrived, (held, sem) = refs[:count], refs[count:]
    straight = (arrived[:CHUNKS], arrived[CHUNKS : 2 * CHUNKS])
    onward = (arrived[2 * CHUNKS : 3 * CHUNKS - 1], arrived[3 * CHUNKS - 1 :])
    inst = lax.axis_index("inst")

    def fetch(way, chunk, ref, target):
        first = sum(items[:chunk])

        def one(i, carry):
            code = plan[TARGET + way * LIST + first + i]
            inside = lax.bitwise_and(code, 63)

            @pl.when(lax.shift_right_arithmetic(code, 6) == target)
            def _():
                place = lax.shift_right_logical(inside, 4)
                c = lax.bitwise_and(inside, 15)
                pltpu.make_async_copy(ref.at[i], held.at[c, place], sem.at[c, place]).start()

            return carry

        lax.fori_loop(0, items[chunk], one, 0)

    for way, target in ((0, 0), (1, 2)):

        @pl.when(inst == target)
        def _(way=way, target=target):
            for chunk in range(CHUNKS):
                fetch(way, chunk, straight[way][chunk], target)

    @pl.when(inst == 1)
    def _():
        for way in range(2):
            for chunk in range(CHUNKS - 1):
                fetch(way, chunk, onward[way][chunk], 1)

    for j in range(MOVED):

        def wait(c, carry, j=j):
            pltpu.make_async_copy(held.at[c, j], held.at[c, j], sem.at[c, j]).wait()
            return carry

        lax.fori_loop(0, plan[COUNT + j], wait, 0)


def gather(items, plan, arrived):
    return pl.pallas_call(
        functools.partial(gather_kernel, items),
        out_shape=jax.ShapeDtypeStruct((CTX, MOVED, 2, BLOCK, FEATURES), BF16),
        in_specs=[SMEM] + [ANY] * len(arrived),
        out_specs=VMEM,
        scratch_shapes=[pltpu.SemaphoreType.DMA((CTX, MOVED))],
        cost_estimate=pl.CostEstimate(flops=0, bytes_accessed=8 * 1024 * 1024, transcendentals=0),
        compiler_params=params(12),
        name="gather",
    )(plan, *arrived)


def merge_kernel(parts, out):
    blocks = [parts[d].astype(F32) for d in range(CTX)]
    peaks = []
    totals = []
    for block in blocks:
        stat = block[STAT_ROW : STAT_ROW + 8]
        peaks.append(stat[0:1] + stat[1:2] + stat[2:3])
        totals.append(stat[3:4] + stat[4:5])
    peak = functools.reduce(jnp.maximum, peaks)
    factors = [jnp.exp(p - peak) for p in peaks]
    total = functools.reduce(jnp.add, [f * t for f, t in zip(factors, totals)])
    under = to_rows(jnp.where(total > 0, total, 1.0), HALF_ROWS)
    mixed = functools.reduce(
        jnp.add, [to_rows(f, HALF_ROWS) * b for f, b in zip(factors, blocks)]
    )
    attended = (mixed / under).astype(BF16)
    for d in range(CTX):
        out[d] = attended


def merge(parts):
    return pl.pallas_call(
        merge_kernel,
        out_shape=jax.ShapeDtypeStruct(parts.shape, BF16),
        in_specs=[VMEM],
        out_specs=VMEM,
        compiler_params=params(8),
        name="merge",
    )(parts)


def place_kernel(
    plan, within, received, cache, own, by0, by1, by2, new_cache, out, fixed, empty, sent, sem
):
    ctx = lax.axis_index("ctx")
    empty[...] = jnp.zeros_like(empty)
    sent[...] = by0[...].astype(F32) + by1[...].astype(F32) + by2[...].astype(F32)
    row = lax.broadcasted_iota(I32, (SLOTS, 1), 0)
    request = jnp.full((SLOTS, 1), -1, I32)
    for s in range(SLOTS):
        request = jnp.where(row == s, plan[REQUEST + s], request)
    stays = jnp.where(lax.axis_index("inst") == INST - 1, 0.0, 1.0)
    for t in range(STEPS):
        rows = own[t * SLOTS : (t + 1) * SLOTS, 1024:].astype(F32) * stays
        for r in range(SLOTS):
            at = t * SLOTS + r
            rows = jnp.where(request == r, sent[at : at + 1, 1024:], rows)
        out[t * SLOTS : (t + 1) * SLOTS, :] = rows

    for j in range(MOVED):

        @pl.when(plan[VALID + j] > 0)
        def _(j=j):
            slot = plan[SLOT + j]
            length = plan[LENGTH + j]
            r = plan[REQUEST + slot]

            def one(d, carry):
                b = within[d]
                start = (ctx * CTX + b) * BLOCK
                rows = pl.ds(pl.multiple_of(b * BLOCK, BLOCK), BLOCK)
                target = new_cache.at[:, slot, rows, :]

                @pl.when(start + BLOCK <= length)
                def _():
                    pltpu.make_async_copy(received.at[d, j], target, sem.at[j]).start()

                @pl.when(start >= length + STEPS)
                def _():
                    pltpu.make_async_copy(empty, target, sem.at[j]).start()

                @pl.when(jnp.logical_and(start + BLOCK > length, start < length + STEPS))
                def _():
                    at = start + lax.broadcasted_iota(I32, (BLOCK, 1), 0)
                    half = lax.bitwise_and(b, 1)
                    for kv in range(2):
                        block = jnp.where(at < length, received[d, j, kv], jnp.zeros((), BF16))
                        for t in range(STEPS):
                            new = sent[pl.ds(t * SLOTS + r, 1), kv * 512 : (kv + 1) * 512]
                            block = jnp.where(at == length + t, new.astype(BF16), block)
                        fixed[j, half, kv] = block
                    pltpu.make_async_copy(fixed.at[j, half], target, sem.at[j]).start()

                return carry

            lax.fori_loop(0, CTX, one, 0)

    for j in range(MOVED):

        @pl.when(plan[VALID + j] > 0)
        def _(j=j):
            whole = new_cache.at[:, plan[SLOT + j]]
            pltpu.make_async_copy(whole, whole, sem.at[j]).wait()


def place(plan, within, received, cache, own, by):
    return pl.pallas_call(
        place_kernel,
        out_shape=[
            jax.ShapeDtypeStruct(cache.shape, BF16),
            jax.ShapeDtypeStruct((24, 256), F32),
        ],
        in_specs=[SMEM, SMEM, VMEM, HBM] + [VMEM] * 4,
        out_specs=[HBM, VMEM],
        scratch_shapes=[
            pltpu.VMEM((MOVED, 2, 2, BLOCK, FEATURES), BF16),
            pltpu.VMEM((2, BLOCK, FEATURES), BF16),
            pltpu.VMEM((24, 1280), F32),
            pltpu.SemaphoreType.DMA((MOVED,)),
        ],
        input_output_aliases={3: 0},
        compiler_params=params(12),
        name="place",
    )(plan, within, received, cache, own, *by)


def swap(x):
    return lax.all_to_all(x, "ctx", split_axis=0, concat_axis=0, tiled=True)


def after(*values):
    return lax.optimization_barrier(values)


def shards(
    cache,
    hidden,
    norm_gain,
    w_query,
    key_value_weight,
    w_out,
    lengths,
    dest_inst,
    dest_slot,
    block_order,
):
    plan = make_plan(lengths, dest_inst, dest_slot, block_order)
    operands = (
        plan, cache, hidden, norm_gain[None], w_query, key_value_weight, w_out, lengths,
        block_order,
    )
    return lax.switch(
        plan[NEED], [functools.partial(decode, items) for items in ITEMS], *operands
    )


def angles(lengths):
    own = lax.dynamic_slice_in_dim(lengths, lax.axis_index("inst") * SLOTS, SLOTS)
    token = own[None, :] + jnp.arange(STEPS, dtype=I32)[:, None]
    half = HEAD_SIZE // 2
    frequency = ROPE_BASE ** (-jnp.arange(half, dtype=F32) * 2.0 / HEAD_SIZE)
    angle = token.astype(F32).reshape(24, 1) * frequency
    is_value = lax.axis_index("ctx") >= 14
    cosine = jnp.where(is_value, 1.0, jnp.cos(angle))
    sine = jnp.where(is_value, 0.0, jnp.sin(angle))
    return jnp.concatenate([cosine, cosine], axis=1), jnp.concatenate([-sine, sine], axis=1)


def up(x):
    return lax.ppermute(x, "inst", [(INST - 1, 0)])


def down(x):
    return lax.ppermute(x, "inst", [(INST - 1, 2)])


def pass_on(from_up, from_down):
    return lax.ppermute(from_up, "inst", [(0, 1)]), lax.ppermute(from_down, "inst", [(2, 1)])


def decode(items, plan, cache, hidden, gain, w_query, w_kv, w_out, lengths, order):
    packed_up, packed_down = pack(0, items[0], plan, cache)
    up_0, down_0 = up(packed_up), down(packed_down)
    first = lax.axis_index("head") == 0
    hidden, lengths, packed_up, first = after(hidden, lengths, packed_up, first)
    cosine, sine = angles(lengths)
    projected, within = project(hidden, order, gain, w_query, w_kv)
    projected, cosine, sine, plan = after(projected, cosine, sine, plan)
    packed_up, packed_down = pack(items[0], items[1], plan, cache)
    parts, packed_up, packed_down = after(swap(projected), packed_up, packed_down)
    up_1, down_1 = up(packed_up), down(packed_down)
    turned = swap(rotate(parts, cosine, sine))
    turned = turned.reshape(32, STEPS, SLOTS, HEAD_SIZE)
    query = turned[:24].reshape(2, 12, STEPS, SLOTS, HEAD_SIZE).transpose(3, 0, 1, 2, 4)
    query = query.reshape(SLOTS, 2, 36, HEAD_SIZE)
    query = jnp.pad(query, ((0, 0), (0, 0), (0, HALF_ROWS - 36), (0, 0)))
    query = query.reshape(SLOTS, 2 * HALF_ROWS, HEAD_SIZE)
    rows = turned[24:].reshape(8, 24, HEAD_SIZE).transpose(1, 0, 2).reshape(24, 1024)
    entries = rows.reshape(STEPS, SLOTS, 2, FEATURES).transpose(1, 2, 0, 3)
    entries = jnp.pad(entries, ((0, 0), (0, 0), (0, 8 - STEPS), (0, 0)))

    new_cache, sums = attend_slots(lengths, order, cache, query, entries)
    sums, up_0, down_0 = after(sums, up_0, down_0)
    up_on, down_on = pass_on(up_0, down_0)
    attended = swap(merge(swap(sums.reshape(CTX, HALF_ROWS, HEAD_SIZE))))
    attended = attended[:, :36].reshape(SLOTS, 2, 12, STEPS, HEAD_SIZE)
    attended = attended.transpose(3, 0, 1, 2, 4).reshape(24, 24 * HEAD_SIZE)
    projected = jnp.dot(attended, w_out, preferred_element_type=F32)
    projected, up_1 = after(projected, up_1)
    held = gather(items, plan, [up_0, up_1, down_0, down_1, up_on, down_on])
    mine, other = projected[:, :192], projected[:, 192:]
    keep = jnp.where(first, mine, other)
    send_half = jnp.where(first, other, mine).astype(BF16)
    got = lax.ppermute(send_half, "head", [(0, 1), (1, 0)])
    attn_out = (keep + got.astype(F32)).astype(BF16)
    own = jnp.concatenate([rows, attn_out, jnp.zeros((24, 64), BF16)], axis=1)
    by = [lax.ppermute(own, "inst", [(INST - 1, i)]) for i in range(INST - 1)]
    *by, own, held = after(*by, own, held)
    new_cache, attn_out = place(plan, within, swap(held), new_cache, own, by)
    attn_out = attn_out[:, :192].astype(BF16)
    return new_cache, attn_out.reshape(STEPS, SLOTS, 192)


def solution(mesh):
    placed = (
        P(None, "inst", "ctx", "head"),
        P(None, "inst", "ctx"),
        P("ctx"),
        P("ctx", "head"),
        P(None, "ctx", "head"),
        P("head", "ctx"),
        P(),
        P(),
        P(),
        P(),
    )
    return jax.shard_map(
        shards,
        mesh=mesh,
        in_specs=placed,
        out_specs=(P(None, "inst", "ctx", "head"), P(None, "inst", ("ctx", "head"))),
        check_vma=False,
    )
```
